256 devices in a mesh: panel: 2 (over core), rad: 4 (over z_lo), hor: 32 (over y, x, z_hi).
Axes of the slice: x: 4, y: 4, z: 8 (z_hi: 2, z_lo: 4; z = z_hi * 4 + z_lo), core: 2. Of those that a mesh axis runs over, the one named last changes fastest.
Arguments:
- final_cotangent: float32 [2, 8, 4, 256, 2304], P('panel', None, 'rad', 'hor'), may hold values from -6 to 6
- diffusivity: float32 [2, 4, 256, 2304], P('panel', 'rad', 'hor'), may hold values from 0.3 to 1.5
- theta_velocity: float32 [2, 4, 256, 2304], P('panel', 'rad', 'hor'), may hold values from -2.5 to 2.5
- phi_velocity: float32 [2, 4, 256, 2304], P('panel', 'rad', 'hor'), may hold values from -2.5 to 2.5
- radial_stencil: float32 [3, 8, 4], replicated, may hold values from -1 to 1
- field_coupling: float32 [4, 8, 8], replicated, may hold values from -2.5 to 2.5
- slot_targets: int32 [2, 32, 896], P('panel', 'hor'), may hold values from 0 to 5119, as said below
- slot_donors: int32 [2, 32, 896], P('panel', 'hor'), may hold values from 0 to 18431, as said below
- slot_weights: float32 [2, 32, 896], P('panel', 'hor'), may hold values from 0.1 to 0.4
- slot_counts: int32 [2, 32], P('panel', 'hor'), may hold values from 576 to 832, as said below
Outputs:
- initial_adjoint: float32 [2, 8, 4, 256, 2304], P('panel', None, 'rad', 'hor')
The draws below stay inside these ranges and needn't reach their ends.
Inputs may be any that keep to these rules, and one draw needn't show every extreme that they name: `slot_targets`: each cell of the first and last rows of a panel is the target of four slots, all in the list of the donor tile s whose index times 2304 / 32 is at most its column and whose next index times 2304 / 32 is above it; each cell of the first and last columns is the target of four slots in the list of one donor tile, and 8 consecutive donor tiles, starting at a tile drawn for each panel, hold these, each for 32 rows in order; live slots come first, the four slots of a cell side by side. `slot_donors`: the four donors of a cell are the corners of a two by two block of cells of one donor tile; for the first cell of every list this block is the tile's last two rows and last two columns. `slot_counts`: A donor tile's list holds 576 live slots, plus 32 * 8 if it is one of the 8 tiles that hold the first and last columns' cells.
All inputs are finite; a program needn't handle non-finite values.
Results may differ from the reference program's by a relative error of at most 0.00005.
Values sent between devices are 32-bit elements; how exact they have to be, the bound alone decides.
A program may use at most 128 MiB of HBM per device.

```python
import math
import jax
import jax.numpy as jnp
from jax import lax

FIELDS = 8
ROWS_DEV = 8
PH = 2304
LEVELS = 4
TILES = 32
TH = 256
SLOTS = 896


def slot_plan(key):
    keys = jax.random.split(jax.random.fold_in(key, 7), 3)
    per_tile = PH // TILES
    band = TILES // 4
    edge_slots = 8 * per_tile
    side_slots = 32 * ROWS_DEV
    band_rows = 4 * ROWS_DEV
    start = jax.random.randint(keys[0], (2, 1), 0, TILES - band + 1).astype(jnp.int32)
    tile = jnp.arange(TILES, dtype=jnp.int32)[None, :]
    in_band = (tile >= start) & (tile < start + band)
    counts = (edge_slots + jnp.where(in_band, side_slots, 0)).astype(jnp.int32)
    slot_ids = jnp.arange(SLOTS, dtype=jnp.int32)[None, None, :]
    cell = slot_ids // 4
    corner = slot_ids % 4
    edge_row = cell // per_tile
    edge_col = tile[..., None] * per_tile + cell % per_tile
    edge_position = edge_row * PH + edge_col
    side_index = (slot_ids - edge_slots) // 4
    side = side_index // band_rows
    global_row = (tile - start)[..., None] * band_rows + side_index % band_rows
    side_position = 2 * PH + side * TH + global_row
    live = slot_ids < counts[..., None]
    targets = jnp.where(live, jnp.where(slot_ids < edge_slots, edge_position, side_position), 0).astype(jnp.int32)
    image_row = jnp.repeat(jax.random.randint(keys[1], (2, TILES, SLOTS // 4), 0, ROWS_DEV - 1), 4, axis=2)
    image_col = jnp.repeat(jax.random.randint(keys[2], (2, TILES, SLOTS // 4), 0, PH - 1), 4, axis=2)
    image_row = jnp.where(slot_ids < 4, ROWS_DEV - 2, image_row).astype(jnp.int32)
    image_col = jnp.where(slot_ids < 4, PH - 2, image_col).astype(jnp.int32)
    donors = jnp.where(live, (image_row + corner // 2) * PH + image_col + corner % 2, 0).astype(jnp.int32)
    return (targets, donors, counts)


def draw_slot_targets(key, part):
    return slot_plan(key)[0]


def draw_slot_donors(key, part):
    return slot_plan(key)[1]


def draw_slot_counts(key, part):
    return slot_plan(key)[2]


def steps_of(own_key, shape, pieces, least, high):
    loudness, own = 1.0, jax.random.fold_in(own_key, 6)
    for axis_at, blocks in pieces:
        steps = jnp.exp(jax.random.uniform(jax.random.fold_in(own, axis_at), (blocks,), jnp.float32, least / len(pieces), high / len(pieces)))
        loudness = loudness * jnp.repeat(steps, shape[axis_at] // blocks).reshape([-1 if axis == axis_at else 1 for axis in range(len(shape))])
    return loudness


def centred(own_key, extent, deviation, most, shards=(), held_as=jnp.bfloat16):
    drawn = deviation * jax.random.normal(own_key, extent, jnp.float32)
    if shards:
        drawn = drawn * steps_of(own_key, extent, shards, -0.22, 0.18)
    return jnp.clip(drawn, -most, most).astype(held_as)


def setup_inputs(seed: int = 0) -> dict:
    seeds = jax.random.split(jax.random.key(seed), 11)
    return {
        "final_cotangent": centred(seeds[0], (2, FIELDS, LEVELS, TH, PH), 1.0, 6.0, ((0, 2), (2, 4), (3, 32)), jnp.float32),
        "diffusivity": jnp.clip(jnp.exp(math.log(1.5) - 1.60943787 * jax.random.uniform(seeds[1], (2, LEVELS, TH, PH), jnp.float32) ** steps_of(seeds[1], (2, LEVELS, TH, PH), ((0, 2), (1, 4), (2, 32)), -0.2, 0.2)), 0.3, 1.5),
        "theta_velocity": centred(seeds[2], (2, LEVELS, TH, PH), 0.5, 2.5, ((0, 2), (1, 4), (2, 32)), jnp.float32),
        "phi_velocity": centred(seeds[3], (2, LEVELS, TH, PH), 0.5, 2.5, ((0, 2), (1, 4), (2, 32)), jnp.float32),
        "radial_stencil": jnp.clip(jax.random.uniform(seeds[4], (3, FIELDS, LEVELS), jnp.float32, -1.0, 1.0), -1.0, 1.0),
        "field_coupling": centred(seeds[5], (LEVELS, FIELDS, FIELDS), 0.35, 2.5, (), jnp.float32),
        "slot_targets": draw_slot_targets(jax.random.fold_in(seeds[10], 71), 0),
        "slot_donors": draw_slot_donors(jax.random.fold_in(seeds[10], 71), 0),
        "slot_weights": jnp.clip(0.1 + 0.3 * jax.random.uniform(seeds[8], (2, TILES, SLOTS), jnp.float32) ** steps_of(seeds[8], (2, TILES, SLOTS), ((0, 2), (1, 32)), -0.2, 0.2), 0.1, 0.4),
        "slot_counts": draw_slot_counts(jax.random.fold_in(seeds[10], 71), 0),
    }


STEP_SIZE = 0.2

def from_lower(field, axis):
    widths = [(0, 0)] * field.ndim
    widths[axis] = (1, 0)
    return lax.slice_in_dim(jnp.pad(field, widths), 0, field.shape[axis], axis=axis)

def from_upper(field, axis):
    widths = [(0, 0)] * field.ndim
    widths[axis] = (0, 1)
    return lax.slice_in_dim(jnp.pad(field, widths), 1, field.shape[axis] + 1, axis=axis)

def operator(state, diffusivity, theta_velocity, phi_velocity, radial_stencil, field_coupling):
    diffuse = diffusivity[:, None]
    theta_flow = theta_velocity[:, None]
    phi_flow = phi_velocity[:, None]
    horizontal = from_lower((diffuse + theta_flow) * state, 3) + from_upper((diffuse - theta_flow) * state, 3)
    horizontal = horizontal + from_lower((diffuse + phi_flow) * state, 4) + from_upper((diffuse - phi_flow) * state, 4)
    horizontal = horizontal - 4.0 * diffuse * state
    diagonal = radial_stencil[0][None, :, :, None, None]
    upper = radial_stencil[1][None, :, :, None, None]
    lower = radial_stencil[2][None, :, :, None, None]
    radial = diagonal * state + upper * from_upper(state, 2) + lower * from_lower(state, 2)
    coupled = jnp.einsum('rfe,perij->pfrij', field_coupling, state, precision=lax.Precision.HIGHEST)
    return horizontal + radial + coupled

def overset(state, border, target_flat, donor_global, live_weights):
    flat = state.reshape(2, FIELDS, LEVELS, TH * PH)
    added = []
    for receiving in range(2):
        donor_panel = 1 - receiving
        values = flat[donor_panel][:, :, donor_global[donor_panel].reshape(-1)] * live_weights[donor_panel].reshape(-1)
        filled = jnp.zeros((FIELDS, LEVELS, TH * PH), jnp.float32).at[:, :, target_flat[donor_panel].reshape(-1)].add(values)
        added.append(filled)
    return jnp.where(border, jnp.float32(0.0), state) + jnp.stack(added).reshape(state.shape)

def reference(final_cotangent, diffusivity, theta_velocity, phi_velocity, radial_stencil, field_coupling, slot_targets, slot_donors, slot_weights, slot_counts):
    row_ids = jnp.arange(TH, dtype=jnp.int32)[:, None]
    col_ids = jnp.arange(PH, dtype=jnp.int32)[None, :]
    border = (row_ids == 0) | (row_ids == TH - 1) | (col_ids == 0) | (col_ids == PH - 1)
    tile_cells = ROWS_DEV * PH
    tile_ids = jnp.arange(TILES, dtype=jnp.int32)
    position = slot_targets.astype(jnp.int32)
    target_row = jnp.where(position < PH, 0, jnp.where(position < 2 * PH, TH - 1, jnp.where(position < 2 * PH + TH, position - 2 * PH, position - 2 * PH - TH))).astype(jnp.int32)
    target_col = jnp.where(position < PH, position, jnp.where(position < 2 * PH, position - PH, jnp.where(position < 2 * PH + TH, 0, PH - 1))).astype(jnp.int32)
    target_flat = (target_row * PH + target_col).astype(jnp.int32)
    donor_global = (tile_ids[None, :, None] * tile_cells + slot_donors).astype(jnp.int32)
    live = jnp.arange(SLOTS, dtype=jnp.int32)[None, None, :] < slot_counts[..., None]
    live_weights = jnp.where(live, slot_weights, jnp.float32(0.0))

    def apply_operator(state):
        return operator(state, diffusivity, theta_velocity, phi_velocity, radial_stencil, field_coupling)

    def apply_overset(state):
        return overset(state, border, target_flat, donor_global, live_weights)

    def forward(initial):
        halfway = apply_overset(initial + 0.5 * STEP_SIZE * apply_operator(initial))
        return apply_overset(initial + STEP_SIZE * apply_operator(halfway))
    _, pullback = jax.vjp(forward, jnp.zeros_like(final_cotangent))
    return pullback(final_cotangent)[0]
```

```python
import functools

import jax
import jax.numpy as jnp
from jax import lax
from jax.experimental import pallas as pl
from jax.experimental.pallas import tpu as pltpu
from jax.sharding import PartitionSpec as P

STEP_SIZE = 0.2
MESH = pl.DeviceIdType.MESH
F32 = jnp.float32
BF16 = jnp.bfloat16
BLK = 256


def split(x):
    hi = x.astype(BF16)
    lo = (x - hi.astype(F32)).astype(BF16)
    return hi, lo


def kernel(
    tiles,
    levels,
    c_ref,
    kap_ref,
    vt_ref,
    vp_ref,
    rs_ref,
    fc_ref,
    tgt_ref,
    don_ref,
    wt_ref,
    cnt_ref,
    out_ref,
    w_ref,
    v_ref,
    rad_buf,
    hal_send,
    hal_recv,
    side_msg,
    side_buf,
    row_line,
    pieces,
    row_buf,
    val_send,
    val_recv,
    gather_rows,
    gather_sides,
    side_group,
    key_ref,
    live_ref,
    lane_hot,
    spread,
    own_part,
    rad_part,
    rad_ssem,
    rad_rsem,
    hal_ssem,
    hal_rsem,
    side_ssem,
    side_rsem,
    piece_ssem,
    piece_rsem,
    val_ssem,
    val_rsem,
):
    fields, rows, columns = c_ref.shape
    slots = key_ref.shape[1]
    per_tile = columns // tiles
    nblk = columns // BLK
    panel = lax.axis_index("panel")
    rad = lax.axis_index("rad")
    hor = lax.axis_index("hor")
    other = 1 - panel

    barrier = pltpu.get_barrier_semaphore()

    def greet(j, carry):
        pl.semaphore_signal(
            barrier, inc=1, device_id={"panel": other, "hor": j}, device_id_type=MESH
        )
        return carry

    lax.fori_loop(0, tiles, greet, 0)

    has_low, has_high = rad > 0, rad < levels - 1
    has_north, has_south = hor > 0, hor < tiles - 1

    def to_rad(step):
        return {"rad": rad + step}

    def to_hor(step):
        return {"hor": hor + step}

    around = (
        (has_low, to_rad(-1)),
        (has_high, to_rad(1)),
        (has_north, to_hor(-1)),
        (has_south, to_hor(1)),
    )
    for present, where in around:

        @pl.when(present)
        def _():
            pl.semaphore_signal(barrier, inc=1, device_id=where, device_id_type=MESH)

    row_ids = lax.broadcasted_iota(jnp.int32, (rows, BLK), 0)
    lane_ids = lax.broadcasted_iota(jnp.int32, (rows, BLK), 1)
    bad_row = ((row_ids == 0) & (hor == 0)) | ((row_ids == rows - 1) & (hor == tiles - 1))

    def border_mask(block):
        col = lane_ids + block * BLK
        return bad_row | (col == 0) | (col == columns - 1)

    def rad_copy(ph, src, up):
        slot = 0 if up else 1
        return pltpu.make_async_remote_copy(
            src_ref=src,
            dst_ref=rad_buf.at[ph, slot],
            send_sem=rad_ssem.at[ph, slot],
            recv_sem=rad_rsem.at[ph, slot],
            device_id=to_rad(1 if up else -1),
            device_id_type=MESH,
        )

    def val_copy(ph, up):
        slot = 0 if up else 1
        return pltpu.make_async_remote_copy(
            src_ref=val_send.at[ph],
            dst_ref=val_recv.at[ph, slot],
            send_sem=val_ssem.at[ph, slot],
            recv_sem=val_rsem.at[ph, slot],
            device_id=to_rad(1 if up else -1),
            device_id_type=MESH,
        )

    def hal_copy(ph, down):
        slot = 0 if down else 1
        return pltpu.make_async_remote_copy(
            src_ref=hal_send.at[ph, slot],
            dst_ref=hal_recv.at[ph, slot],
            send_sem=hal_ssem.at[ph, slot],
            recv_sem=hal_rsem.at[ph, slot],
            device_id=to_hor(1 if down else -1),
            device_id_type=MESH,
        )

    def side_copy(ph, j):
        return pltpu.make_async_remote_copy(
            src_ref=side_msg.at[ph],
            dst_ref=side_buf.at[ph, hor],
            send_sem=side_ssem.at[ph],
            recv_sem=side_rsem.at[ph],
            device_id={"panel": other, "hor": j},
            device_id_type=MESH,
        )

    def sides_all(ph):
        return pltpu.make_async_remote_copy(
            src_ref=side_buf.at[ph],
            dst_ref=side_buf.at[ph],
            send_sem=side_ssem.at[ph],
            recv_sem=side_rsem.at[ph],
            device_id={"panel": other},
            device_id_type=MESH,
        )

    def piece_copy(ph, edge, j):
        return pltpu.make_async_remote_copy(
            src_ref=pieces.at[ph, j],
            dst_ref=row_buf.at[ph, edge],
            send_sem=piece_ssem.at[ph],
            recv_sem=piece_rsem.at[ph, edge],
            device_id={"panel": other, "hor": j},
            device_id_type=MESH,
        )

    def pieces_all(ph):
        return pltpu.make_async_remote_copy(
            src_ref=pieces.at[ph],
            dst_ref=pieces.at[ph],
            send_sem=piece_ssem.at[ph],
            recv_sem=piece_rsem.at[ph, 0],
            device_id={"panel": other},
            device_id_type=MESH,
        )

    def pack_border(ph, src):
        lanes = lax.broadcasted_iota(jnp.int32, (rows, 128), 1)
        both = jnp.zeros((rows, 128), F32)
        for f in range(fields):
            first = src[f, :, 0:1]
            last = src[f, :, columns - 1 : columns]
            both = jnp.where(lanes == f, first, both)
            both = jnp.where(lanes == fields + f, last, both)
        turned = pltpu.roll(both, 0, 1, stride=2 * fields, stride_axis=0)
        side_msg[ph] = jnp.sum(turned, axis=0, keepdims=True)

        for edge, row, here in ((0, 0, hor == 0), (1, rows - 1, hor == tiles - 1)):

            @pl.when(here)
            def _():
                for f in range(fields):
                    row_line[f : f + 1, 0:columns] = src[f, row : row + 1, :]
                row_line[:, columns : columns + 128] = jnp.zeros((fields, 128), F32)
                for j in range(tiles):
                    base, off = divmod(per_tile * j, 128)
                    one = row_line[:, base * 128 : base * 128 + 128]
                    if off:
                        two = row_line[:, base * 128 + 128 : base * 128 + 256]
                        one = pltpu.roll(one, 128 - off, 1)
                        two = pltpu.roll(two, 128 - off, 1)
                        one = jnp.where(lanes < 128 - off, one, two)
                    pieces[ph, j] = one

    def send_border(ph):
        def one(j, carry):
            side_copy(ph, j).start()
            return carry

        lax.fori_loop(0, tiles, one, 0)
        for edge, here in ((0, hor == 0), (1, hor == tiles - 1)):

            @pl.when(here)
            def _():
                def row(j, carry):
                    piece_copy(ph, edge, j).start()
                    return carry

                lax.fori_loop(0, tiles, row, 0)

    def send_rad(ph, src):
        @pl.when(has_high)
        def _():
            rad_copy(ph, src, True).start()

        @pl.when(has_low)
        def _():
            rad_copy(ph, src, False).start()

    def prepare():
        tgt = tgt_ref[0]
        don = don_ref[0]
        slot_ids = lax.broadcasted_iota(jnp.int32, (1, slots), 1)
        live_ref[...] = jnp.where(slot_ids < cnt_ref[...], wt_ref[0], F32(0.0))
        first = tgt - per_tile * hor
        second = tgt - columns - per_tile * hor
        entry = jnp.where(
            tgt < columns, first, jnp.where(tgt < 2 * columns, second + 128, -1)
        )
        ids = lax.broadcasted_iota(jnp.int32, (BLK, slots), 0)
        gather_rows[...] = jnp.where(ids == entry, F32(1), F32(0)).astype(BF16)
        place = tgt - 2 * columns
        far = jnp.where(place >= tiles * rows, 1, 0)
        line = place - far * (tiles * rows)
        tile = jnp.where(place >= 0, line >> 3, -1)
        hids = lax.broadcasted_iota(jnp.int32, (tiles, slots), 0)
        gather_sides[...] = jnp.where(hids == tile, F32(1), F32(0)).astype(BF16)
        side_group[...] = 2 * (line & 7) + far
        local = jnp.zeros_like(don)
        for m in range(1, rows):
            local = local + jnp.where(don >= m * columns, 1, 0)
        col = don - local * columns
        key_ref[...] = (col >> 8) * rows + local
        hot = jnp.where(ids == (col & (BLK - 1)), F32(1), F32(0)).astype(BF16)
        lane_hot[:, 0:slots] = hot
        lane_hot[:, slots : 2 * slots] = hot

    def gather(ph):
        table = jnp.concatenate([row_buf[ph, 0], row_buf[ph, 1]], axis=1)
        hi, lo = split(table)
        got = jnp.dot(
            jnp.concatenate([hi, lo], axis=0), gather_rows[...], preferred_element_type=F32
        )
        from_rows = got[0:fields] + got[fields : 2 * fields]
        turned = side_buf[ph, :, 0, :].T
        hi, lo = split(turned)
        got = jnp.dot(
            jnp.concatenate([hi, lo], axis=0), gather_sides[...], preferred_element_type=F32
        )
        got = got[0:128] + got[128:256]
        total = from_rows
        group = side_group[...]
        for g in range(2 * rows):
            part = got[g * fields : (g + 1) * fields]
            total = total + jnp.where(group == g, part, F32(0.0))
        return total * live_ref[...]

    def scatter(values, into):
        hi, lo = split(values)
        hi, lo = hi.astype(F32), lo.astype(F32)
        key = key_ref[...]
        own = lax.broadcasted_iota(jnp.int32, (rows, slots), 0)

        def one(block, carry):
            hit = key == own + block * rows
            at = pl.multiple_of(block * (fields * rows), fields * rows)
            for part, x in ((0, hi), (1, lo)):
                picked = [jnp.where(hit, x[f : f + 1], F32(0.0)) for f in range(fields)]
                spread[pl.ds(at, fields * rows), part * slots : (part + 1) * slots] = (
                    jnp.concatenate(picked, axis=0).astype(BF16)
                )
            return carry

        lax.fori_loop(0, nblk, one, 0)
        into[...] = lax.dot_general(
            spread[...], lane_hot[...], (((1,), (1,)), ((), ())), preferred_element_type=F32
        )

    def coefficients(f):
        low = rs_ref[1, f, jnp.maximum(rad - 1, 0)]
        high = rs_ref[2, f, jnp.minimum(rad + 1, levels - 1)]
        low = jnp.where(has_low, low, F32(0.0))
        high = jnp.where(has_high, high, F32(0.0))
        return low, high

    def overset(ph, src):
        sides_all(ph).wait_recv()
        piece_copy(ph, 0, 0).wait_recv()
        piece_copy(ph, 1, 0).wait_recv()
        values = gather(ph)
        val_send[ph] = values

        @pl.when(has_high)
        def _():
            val_copy(ph, True).start()

        @pl.when(has_low)
        def _():
            val_copy(ph, False).start()

        scatter(values, own_part)

        def one(block, carry):
            at = pl.multiple_of(block * BLK, BLK)
            border = border_mask(block)
            for f in range(fields):
                start = pl.multiple_of(block * (fields * rows) + f * rows, rows)
                x = jnp.where(border, F32(0.0), src[f, :, pl.ds(at, BLK)])
                x = x + own_part[pl.ds(start, rows), :]
                v_ref[ph, f, :, pl.ds(at + 128, BLK)] = x
                hal_send[ph, 0, f : f + 1, pl.ds(at, BLK)] = x[rows - 1 : rows]
                hal_send[ph, 1, f : f + 1, pl.ds(at, BLK)] = x[0:1]
            return carry

        lax.fori_loop(0, nblk, one, 0)

        @pl.when(has_south)
        def _():
            hal_copy(ph, True).start()

        @pl.when(has_north)
        def _():
            hal_copy(ph, False).start()

        @pl.when(has_low)
        def _():
            val_copy(ph, True).wait_recv()

        @pl.when(has_high)
        def _():
            val_copy(ph, False).wait_recv()

        mixed = []
        for f in range(fields):
            low, high = coefficients(f)
            mixed.append(
                low * val_recv[ph, 0, f : f + 1, :] + high * val_recv[ph, 1, f : f + 1, :]
            )
        scatter(jnp.concatenate(mixed, axis=0), rad_part)

    def wait_neighbours(ph, src):
        @pl.when(has_low)
        def _():
            rad_copy(ph, src, True).wait_recv()

        @pl.when(has_high)
        def _():
            rad_copy(ph, src, False).wait_recv()

        @pl.when(has_north)
        def _():
            hal_copy(ph, True).wait_recv()

        @pl.when(has_south)
        def _():
            hal_copy(ph, False).wait_recv()

    def wait_sends(ph, src):
        for present, copy in (
            (has_high, lambda: rad_copy(ph, src, True)),
            (has_low, lambda: rad_copy(ph, src, False)),
            (has_high, lambda: val_copy(ph, True)),
            (has_low, lambda: val_copy(ph, False)),
            (has_south, lambda: hal_copy(ph, True)),
            (has_north, lambda: hal_copy(ph, False)),
            ((hor == 0) | (hor == tiles - 1), lambda: pieces_all(ph)),
        ):

            @pl.when(present)
            def _():
                copy().wait_send()

        sides_all(ph).wait_send()

    def operator(ph, finish):
        def one(block, carry):
            at = pl.multiple_of(block * BLK, BLK)
            cols = pl.ds(at, BLK)
            kap = kap_ref[0, 0, :, cols]
            vt = vt_ref[0, 0, :, cols]
            vp = vp_ref[0, 0, :, cols]
            north, south = kap + vt, kap - vt
            east, west = kap + vp, kap - vp
            center = 4.0 * kap
            border = border_mask(block)
            here, total = [], []
            for f in range(fields):
                wide = v_ref[ph, f, :, pl.ds(at, BLK + 256)]
                cur = wide[:, 128 : 128 + BLK]
                before = pltpu.roll(wide, 1, 1)[:, 128 : 128 + BLK]
                after = pltpu.roll(wide, BLK + 255, 1)[:, 128 : 128 + BLK]
                below = jnp.where(
                    row_ids == 0, hal_recv[ph, 0, f : f + 1, cols], pltpu.roll(cur, 1, 0)
                )
                above = jnp.where(
                    row_ids == rows - 1,
                    hal_recv[ph, 1, f : f + 1, cols],
                    pltpu.roll(cur, rows - 1, 0),
                )
                low, high = coefficients(f)
                start = pl.multiple_of(block * (fields * rows) + f * rows, rows)
                mixed = low * rad_buf[ph, 0, f, :, cols] + high * rad_buf[ph, 1, f, :, cols]
                acc = jnp.where(border, F32(0.0), mixed) + rad_part[pl.ds(start, rows), :]
                acc = acc + south * below + north * above + west * before + east * after
                acc = acc - center * cur + rs_ref[0, f, rad] * cur
                here.append(cur)
                total.append(acc)
            for e in range(fields):
                acc = total[e]
                for f in range(fields):
                    acc = acc + fc_ref[rad, f, e] * here[f]
                finish(e, cols, at, here[e], acc)
            return carry

        lax.fori_loop(0, nblk, one, 0)

    pack_border(0, c_ref)
    zero_block = jnp.zeros((2, fields, rows, 128), F32)
    v_ref[:, :, :, 0:128] = zero_block
    v_ref[:, :, :, columns + 128 : columns + 256] = zero_block
    for present, slot in ((has_low, 0), (has_high, 1)):

        @pl.when(jnp.logical_not(present))
        def _():
            for ph in range(2):
                rad_buf[ph, slot] = jnp.zeros(rad_buf.shape[2:], F32)
                val_recv[ph, slot] = jnp.zeros(val_recv.shape[2:], F32)

    for present, slot in ((has_north, 0), (has_south, 1)):

        @pl.when(jnp.logical_not(present))
        def _():
            for ph in range(2):
                hal_recv[ph, slot] = jnp.zeros(hal_recv.shape[2:], F32)

    count = tiles
    for present, _ in around:
        count = count + jnp.where(present, 1, 0)
    pl.semaphore_wait(barrier, count)

    send_rad(0, c_ref)
    send_border(0)
    prepare()
    overset(0, c_ref)
    wait_neighbours(0, c_ref)

    def pulled(e, cols, at, here, acc):
        w_ref[e, :, cols] = STEP_SIZE * acc

    operator(0, pulled)

    send_rad(1, w_ref)
    pack_border(1, w_ref)
    send_border(1)
    overset(1, w_ref)
    wait_neighbours(1, w_ref)

    def final(e, cols, at, here, acc):
        out_ref[e, :, cols] = (
            v_ref[0, e, :, pl.ds(at + 128, BLK)] + here + (0.5 * STEP_SIZE) * acc
        )

    operator(1, final)
    wait_sends(0, c_ref)
    wait_sends(1, w_ref)


def body(
    final_cotangent,
    diffusivity,
    theta_velocity,
    phi_velocity,
    radial_stencil,
    field_coupling,
    slot_targets,
    slot_donors,
    slot_weights,
    slot_counts,
):
    fields, _, rows, columns = final_cotangent.shape[1:]
    tiles, levels = lax.axis_size("hor"), lax.axis_size("rad")
    slots = slot_targets.shape[-1]
    nblk = columns // BLK
    block = (fields, rows, columns)
    vmem = pl.BlockSpec(memory_space=pltpu.VMEM)
    smem = pl.BlockSpec(memory_space=pltpu.SMEM)
    dma = pltpu.SemaphoreType.DMA
    out = pl.pallas_call(
        functools.partial(kernel, tiles, levels),
        out_shape=jax.ShapeDtypeStruct(block, F32),
        in_specs=[vmem, vmem, vmem, vmem, smem, smem, vmem, vmem, vmem, vmem],
        out_specs=vmem,
        scratch_shapes=[
            pltpu.VMEM(block, F32),
            pltpu.VMEM((2, fields, rows, columns + 256), F32),
            pltpu.VMEM((2, 2, *block), F32),
            pltpu.VMEM((2, 2, fields, columns), F32),
            pltpu.VMEM((2, 2, fields, columns), F32),
            pltpu.VMEM((2, 1, 128), F32),
            pltpu.VMEM((2, tiles, 1, 128), F32),
            pltpu.VMEM((fields, columns + 128), F32),
            pltpu.VMEM((2, tiles, fields, 128), F32),
            pltpu.VMEM((2, 2, fields, 128), F32),
            pltpu.VMEM((2, fields, slots), F32),
            pltpu.VMEM((2, 2, fields, slots), F32),
            pltpu.VMEM((BLK, slots), BF16),
            pltpu.VMEM((tiles, slots), BF16),
            pltpu.VMEM((1, slots), jnp.int32),
            pltpu.VMEM((1, slots), jnp.int32),
            pltpu.VMEM((1, slots), F32),
            pltpu.VMEM((BLK, 2 * slots), BF16),
            pltpu.VMEM((nblk * fields * rows, 2 * slots), BF16),
            pltpu.VMEM((nblk * fields * rows, BLK), F32),
            pltpu.VMEM((nblk * fields * rows, BLK), F32),
            dma((2, 2)),
            dma((2, 2)),
            dma((2, 2)),
            dma((2, 2)),
            dma((2,)),
            dma((2,)),
            dma((2,)),
            dma((2, 2)),
            dma((2, 2)),
            dma((2, 2)),
        ],
        compiler_params=pltpu.CompilerParams(
            collective_id=0, has_side_effects=True, vmem_limit_bytes=40 * 2**20
        ),
        cost_estimate=pl.CostEstimate(
            flops=8_000_000, bytes_accessed=1_500_000, transcendentals=0
        ),
    )(
        final_cotangent.reshape(block),
        diffusivity,
        theta_velocity,
        phi_velocity,
        radial_stencil,
        field_coupling,
        slot_targets,
        slot_donors,
        slot_weights,
        slot_counts,
    )
    return out.reshape(final_cotangent.shape)


def solution(mesh):
    return jax.shard_map(
        body,
        mesh=mesh,
        in_specs=(
            P("panel", None, "rad", "hor", None),
            P("panel", "rad", "hor", None),
            P("panel", "rad", "hor", None),
            P("panel", "rad", "hor", None),
            P(),
            P(),
            P("panel", "hor", None),
            P("panel", "hor", None),
            P("panel", "hor", None),
            P("panel", "hor"),
        ),
        out_specs=P("panel", None, "rad", "hor", None),
        check_vma=False,
    )
```

```python
import functools

import jax
import jax.numpy as jnp
from jax import lax
from jax.experimental import pallas as pl
from jax.experimental.pallas import tpu as pltpu
from jax.sharding import PartitionSpec as P

STEP_SIZE = 0.2
MESH = pl.DeviceIdType.MESH
F32 = jnp.float32
BF16 = jnp.bfloat16
BLK = 256


def split(x):
    hi = x.astype(BF16)
    lo = (x - hi.astype(F32)).astype(BF16)
    return hi, lo


def kernel(
    tiles,
    levels,
    chunks,
    c_hbm,
    kap_hbm,
    vt_hbm,
    vp_hbm,
    rs_ref,
    fc_ref,
    tgt_hbm,
    don_hbm,
    wt_hbm,
    cnt_ref,
    out_ref,
    c_ref,
    coef,
    ints,
    wts,
    w_ref,
    v_ref,
    rad_buf,
    hal_send,
    hal_recv,
    side_msg,
    side_buf,
    row_line,
    pieces,
    row_buf,
    val_send,
    val_recv,
    info,
    gather_rows,
    gather_sides,
    side_group,
    key_ref,
    lane_hot,
    spread,
    own_part,
    rad_part,
    hal_part,
    load_sem,
    rad_ssem,
    rad_rsem,
    hal_ssem,
    hal_rsem,
    side_ssem,
    side_rsem,
    piece_ssem,
    piece_rsem,
    val_ssem,
    val_rsem,
    info_ssem,
    info_rsem,
):
    fields, rows, columns = c_ref.shape
    slots = key_ref.shape[2]
    window = row_buf.shape[3]
    per_tile = columns // tiles
    nblk = columns // BLK
    width = columns // chunks
    panel = lax.axis_index("panel")
    rad = lax.axis_index("rad")
    hor = lax.axis_index("hor")
    other = 1 - panel

    barrier = pltpu.get_barrier_semaphore()

    def greet(j, carry):
        pl.semaphore_signal(
            barrier, inc=1, device_id={"panel": other, "hor": j}, device_id_type=MESH
        )
        return carry

    lax.fori_loop(0, tiles, greet, 0)

    has_low, has_high = rad > 0, rad < levels - 1
    has_north, has_south = hor > 0, hor < tiles - 1

    def to_rad(step):
        return {"rad": rad + step}

    def to_hor(step):
        return {"hor": hor + step}

    around = (
        (has_low, to_rad(-1)),
        (has_high, to_rad(1)),
        (has_north, to_hor(-1)),
        (has_south, to_hor(1)),
    )
    for present, where in around:

        @pl.when(present)
        def _():
            pl.semaphore_signal(barrier, inc=1, device_id=where, device_id_type=MESH)

    loads = [
        pltpu.make_async_copy(src, dst, load_sem.at[k])
        for k, (src, dst) in enumerate(
            (
                (c_hbm, c_ref),
                (kap_hbm.at[0, 0], coef.at[0]),
                (vt_hbm.at[0, 0], coef.at[1]),
                (vp_hbm.at[0, 0], coef.at[2]),
                (tgt_hbm, ints.at[0]),
                (don_hbm, ints.at[1]),
                (wt_hbm, wts),
            )
        )
    ]
    for load in loads:
        load.start()

    row_ids = lax.broadcasted_iota(jnp.int32, (rows, BLK), 0)
    lane_ids = lax.broadcasted_iota(jnp.int32, (rows, BLK), 1)
    bad_row = ((row_ids == 0) & (hor == 0)) | ((row_ids == rows - 1) & (hor == tiles - 1))

    def side_mask(block):
        col = lane_ids + block * BLK
        return (col == 0) | (col == columns - 1)

    def remote(src, dst, send, recv, where):
        return pltpu.make_async_remote_copy(
            src_ref=src,
            dst_ref=dst,
            send_sem=send,
            recv_sem=recv,
            device_id=where,
            device_id_type=MESH,
        )

    def rad_copy(ph, src, up, k):
        slot = 0 if up else 1
        cols = pl.ds(k * width, width)
        return remote(
            src.at[:, :, cols],
            rad_buf.at[ph, slot, :, :, cols],
            rad_ssem.at[ph, slot, k],
            rad_rsem.at[ph, slot, k],
            to_rad(1 if up else -1),
        )

    def hal_copy(ph, down, k):
        slot = 0 if down else 1
        cols = pl.ds(k * width, width)
        return remote(
            hal_send.at[ph, slot, :, cols],
            hal_recv.at[ph, slot, :, cols],
            hal_ssem.at[ph, slot, k],
            hal_rsem.at[ph, slot, k],
            to_hor(1 if down else -1),
        )

    def val_copy(ph, up):
        slot = 0 if up else 1
        return remote(
            val_send.at[ph],
            val_recv.at[ph, slot],
            val_ssem.at[ph, slot],
            val_rsem.at[ph, slot],
            to_rad(1 if up else -1),
        )

    def info_copy(down):
        slot = 0 if down else 1
        return remote(
            info.at[0],
            info.at[1 + slot],
            info_ssem.at[slot],
            info_rsem.at[slot],
            to_hor(1 if down else -1),
        )

    def side_copy(ph, j):
        return remote(
            side_msg.at[ph],
            side_buf.at[ph, hor],
            side_ssem.at[ph],
            side_rsem.at[ph],
            {"panel": other, "hor": j},
        )

    def sides_all(ph):
        return remote(
            side_buf.at[ph], side_buf.at[ph], side_ssem.at[ph], side_rsem.at[ph], {"panel": other}
        )

    def piece_copy(ph, edge, j):
        return remote(
            pieces.at[ph, j],
            row_buf.at[ph, edge],
            piece_ssem.at[ph],
            piece_rsem.at[ph, edge],
            {"panel": other, "hor": j},
        )

    def pieces_all(ph):
        return remote(
            pieces.at[ph], pieces.at[ph], piece_ssem.at[ph], piece_rsem.at[ph, 0], {"panel": other}
        )

    def pack_border(ph, src):
        lanes = lax.broadcasted_iota(jnp.int32, (rows, 128), 1)
        both = jnp.zeros((rows, 128), F32)
        for f in range(fields):
            first = src[f, :, 0:1]
            last = src[f, :, columns - 1 : columns]
            both = jnp.where(lanes == f, first, both)
            both = jnp.where(lanes == fields + f, last, both)
        turned = pltpu.roll(both, 0, 1, stride=2 * fields, stride_axis=0)
        side_msg[ph] = jnp.sum(turned, axis=0, keepdims=True)

        for edge, row, here in ((0, 0, hor == 0), (1, rows - 1, hor == tiles - 1)):

            @pl.when(here)
            def _():
                for f in range(fields):
                    row_line[f : f + 1, 128 : 128 + columns] = src[f, row : row + 1, :]
                row_line[:, 0:128] = jnp.zeros((fields, 128), F32)
                row_line[:, columns + 128 : columns + 384] = jnp.zeros((fields, 256), F32)
                for j in range(tiles):
                    base, off = divmod(128 + per_tile * (j - 1), 128)
                    one = row_line[:, base * 128 : base * 128 + window + 128]
                    if off:
                        one = pltpu.roll(one, window + 128 - off, 1)
                    pieces[ph, j] = one[:, 0:window]

    def send_border(ph):
        for edge, here in ((0, hor == 0), (1, hor == tiles - 1)):

            @pl.when(here)
            def _():
                def row(j, carry):
                    piece_copy(ph, edge, j).start()
                    return carry

                lax.fori_loop(0, tiles, row, 0)

        def one(j, carry):
            side_copy(ph, j).start()
            return carry

        lax.fori_loop(0, tiles, one, 0)

    def send_chunk(ph, src, k):
        for present, copy in (
            (has_high, lambda: rad_copy(ph, src, True, k)),
            (has_low, lambda: rad_copy(ph, src, False, k)),
            (has_south, lambda: hal_copy(ph, True, k)),
            (has_north, lambda: hal_copy(ph, False, k)),
        ):

            @pl.when(present)
            def _():
                copy().start()

    def wait_chunk(ph, src, k):
        for present, copy in (
            (has_low, lambda: rad_copy(ph, src, True, k)),
            (has_high, lambda: rad_copy(ph, src, False, k)),
            (has_north, lambda: hal_copy(ph, True, k)),
            (has_south, lambda: hal_copy(ph, False, k)),
        ):

            @pl.when(present)
            def _():
                copy().wait_recv()

    def prepare(which):
        tgt = info[which, 0].astype(jnp.int32)
        don = info[which, 1].astype(jnp.int32)
        at = pl.ds(which * slots, slots)
        first = tgt - per_tile * (hor - 1)
        second = first - columns + window
        entry = jnp.where(tgt < columns, first, jnp.where(tgt < 2 * columns, second, -1))
        ids = lax.broadcasted_iota(jnp.int32, (2 * window, slots), 0)
        gather_rows[:, at] = jnp.where(ids == entry, F32(1), F32(0)).astype(BF16)
        place = tgt - 2 * columns
        far = jnp.where(place >= tiles * rows, 1, 0)
        line = place - far * (tiles * rows)
        tile = jnp.where(place >= 0, line >> 3, -1)
        hids = lax.broadcasted_iota(jnp.int32, (tiles, slots), 0)
        gather_sides[:, at] = jnp.where(hids == tile, F32(1), F32(0)).astype(BF16)
        side_group[:, at] = 2 * (line & 7) + far
        local = jnp.zeros_like(don)
        for m in range(1, rows):
            local = local + jnp.where(don >= m * columns, 1, 0)
        col = don - local * columns
        block = col >> 8
        if which == 0:
            key_ref[which] = block * rows + local
        elif which == 1:
            key_ref[which] = jnp.where(local == rows - 1, block, -1)
        else:
            key_ref[which] = jnp.where(local == 0, block, -1)
        lane = jnp.broadcast_to((col & (BLK - 1)).astype(F32), (8, slots)).T[:, 0:1]
        ids = lax.broadcasted_iota(jnp.int32, (slots, BLK), 1).astype(F32)
        hot = jnp.where(ids == lane, F32(1), F32(0)).astype(BF16)
        lane_hot[which, 0:slots, :] = hot
        lane_hot[which, slots : 2 * slots, :] = hot

    def gather(ph):
        table = jnp.concatenate([row_buf[ph, 0], row_buf[ph, 1]], axis=1)
        hi, lo = split(table)
        got = jnp.dot(
            jnp.concatenate([hi, lo], axis=0), gather_rows[...], preferred_element_type=F32
        )
        total = got[0:fields] + got[fields : 2 * fields]
        turned = side_buf[ph, :, 0, :].T
        hi, lo = split(turned)
        got = jnp.dot(
            jnp.concatenate([hi, lo], axis=0), gather_sides[...], preferred_element_type=F32
        )
        got = got[0:128] + got[128:256]
        group = side_group[...]
        for g in range(2 * rows):
            part = got[g * fields : (g + 1) * fields]
            total = total + jnp.where(group == g, part, F32(0.0))
        return [
            total[:, n * slots : (n + 1) * slots] * info[n, 2] for n in range(3)
        ]

    def scatter(values, into):
        hi, lo = split(values)
        hi, lo = hi.astype(F32), lo.astype(F32)
        key = key_ref[0]
        own = lax.broadcasted_iota(jnp.int32, (rows, slots), 0)

        def one(block, carry):
            hit = key == own + block * rows
            at = pl.multiple_of(block * (fields * rows), fields * rows)
            for part, x in ((0, hi), (1, lo)):
                picked = [jnp.where(hit, x[f : f + 1], F32(0.0)) for f in range(fields)]
                spread[pl.ds(at, fields * rows), part * slots : (part + 1) * slots] = (
                    jnp.concatenate(picked, axis=0).astype(BF16)
                )
            return carry

        lax.fori_loop(0, nblk, one, 0)
        into[...] = jnp.dot(spread[...], lane_hot[0], preferred_element_type=F32)

    def scatter_row(which, values):
        hi, lo = split(values)
        key = key_ref[which]
        both = []
        for x in (hi.astype(F32), lo.astype(F32)):
            picked = [jnp.where(key == b, x, F32(0.0)) for b in range(nblk)]
            both.append(jnp.concatenate(picked, axis=0).astype(BF16))
        hal_part[which - 1] = jnp.dot(
            jnp.concatenate(both, axis=1), lane_hot[which], preferred_element_type=F32
        )

    def coefficients(f):
        low = rs_ref[1, f, jnp.maximum(rad - 1, 0)]
        high = rs_ref[2, f, jnp.minimum(rad + 1, levels - 1)]
        low = jnp.where(has_low, low, F32(0.0))
        high = jnp.where(has_high, high, F32(0.0))
        return low, high

    def overset(ph, src):
        sides_all(ph).wait_recv()
        piece_copy(ph, 0, 0).wait_recv()
        piece_copy(ph, 1, 0).wait_recv()
        values, from_north, from_south = gather(ph)
        val_send[ph] = values

        @pl.when(has_high)
        def _():
            val_copy(ph, True).start()

        @pl.when(has_low)
        def _():
            val_copy(ph, False).start()

        scatter(values, own_part)

        def one(block, carry):
            at = pl.multiple_of(block * BLK, BLK)
            border = bad_row | side_mask(block)
            for f in range(fields):
                start = pl.multiple_of(block * (fields * rows) + f * rows, rows)
                x = jnp.where(border, F32(0.0), src[f, :, pl.ds(at, BLK)])
                v_ref[ph, f, :, pl.ds(at + 128, BLK)] = x + own_part[pl.ds(start, rows), :]
            return carry

        lax.fori_loop(0, nblk, one, 0)
        scatter_row(1, from_north)
        scatter_row(2, from_south)

        @pl.when(has_low)
        def _():
            val_copy(ph, True).wait_recv()

        @pl.when(has_high)
        def _():
            val_copy(ph, False).wait_recv()

        mixed = []
        for f in range(fields):
            low, high = coefficients(f)
            mixed.append(
                low * val_recv[ph, 0, f : f + 1, :] + high * val_recv[ph, 1, f : f + 1, :]
            )
        scatter(jnp.concatenate(mixed, axis=0), rad_part)

    def wait_sends(ph, src):
        for k in range(chunks):
            for present, copy in (
                (has_high, lambda: rad_copy(ph, src, True, k)),
                (has_low, lambda: rad_copy(ph, src, False, k)),
                (has_south, lambda: hal_copy(ph, True, k)),
                (has_north, lambda: hal_copy(ph, False, k)),
            ):

                @pl.when(present)
                def _():
                    copy().wait_send()

        for present, copy in (
            (has_high, lambda: val_copy(ph, True)),
            (has_low, lambda: val_copy(ph, False)),
            ((hor == 0) | (hor == tiles - 1), lambda: pieces_all(ph)),
        ):

            @pl.when(present)
            def _():
                copy().wait_send()

        sides_all(ph).wait_send()

    def operator(ph, k, finish):
        def one(block, carry):
            at = pl.multiple_of(block * BLK, BLK)
            cols = pl.ds(at, BLK)
            kap = coef[0, :, cols]
            vt = coef[1, :, cols]
            vp = coef[2, :, cols]
            north, south = kap + vt, kap - vt
            east, west = kap + vp, kap - vp
            center = 4.0 * kap
            sides = side_mask(block)
            border = bad_row | sides
            here, total = [], []
            for f in range(fields):
                wide = v_ref[ph, f, :, pl.ds(at, BLK + 256)]
                cur = wide[:, 128 : 128 + BLK]
                before = pltpu.roll(wide, 1, 1)[:, 128 : 128 + BLK]
                after = pltpu.roll(wide, BLK + 255, 1)[:, 128 : 128 + BLK]
                line = block * fields + f
                edge = []
                for n in range(2):
                    raw = jnp.where(sides[0:1], F32(0.0), hal_recv[ph, n, f : f + 1, cols])
                    edge.append(raw + hal_part[n, pl.ds(line, 1), :])
                below = jnp.where(row_ids == 0, edge[0], pltpu.roll(cur, 1, 0))
                above = jnp.where(row_ids == rows - 1, edge[1], pltpu.roll(cur, rows - 1, 0))
                low, high = coefficients(f)
                start = pl.multiple_of(block * (fields * rows) + f * rows, rows)
                mixed = low * rad_buf[ph, 0, f, :, cols] + high * rad_buf[ph, 1, f, :, cols]
                acc = jnp.where(border, F32(0.0), mixed) + rad_part[pl.ds(start, rows), :]
                acc = acc + south * below + north * above + west * before + east * after
                acc = acc - center * cur + rs_ref[0, f, rad] * cur
                here.append(cur)
                total.append(acc)
            for e in range(fields):
                acc = total[e]
                for f in range(fields):
                    acc = acc + fc_ref[rad, f, e] * here[f]
                finish(e, cols, at, here[e], acc)
            return carry

        each = nblk // chunks
        lax.fori_loop(k * each, (k + 1) * each, one, 0)

    zero_block = jnp.zeros((2, fields, rows, 128), F32)
    v_ref[:, :, :, 0:128] = zero_block
    v_ref[:, :, :, columns + 128 : columns + 256] = zero_block
    for present, slot in ((has_low, 0), (has_high, 1)):

        @pl.when(jnp.logical_not(present))
        def _():
            for ph in range(2):
                rad_buf[ph, slot] = jnp.zeros(rad_buf.shape[2:], F32)
                val_recv[ph, slot] = jnp.zeros(val_recv.shape[2:], F32)

    for present, slot in ((has_north, 0), (has_south, 1)):

        @pl.when(jnp.logical_not(present))
        def _():
            info[1 + slot] = jnp.zeros(info.shape[1:], F32)
            for ph in range(2):
                hal_recv[ph, slot] = jnp.zeros(hal_recv.shape[2:], F32)

    for load in loads:
        load.wait()
    slot_ids = lax.broadcasted_iota(jnp.int32, (1, slots), 1)
    info[0, 0] = ints[0, 0].astype(F32)
    info[0, 1] = ints[1, 0].astype(F32)
    info[0, 2] = jnp.where(slot_ids < cnt_ref[0, 0], wts[0], F32(0.0))
    for f in range(fields):
        hal_send[0, 0, f : f + 1, :] = c_ref[f, rows - 1 : rows, :]
        hal_send[0, 1, f : f + 1, :] = c_ref[f, 0:1, :]
    pack_border(0, c_ref)

    count = tiles
    for present, _ in around:
        count = count + jnp.where(present, 1, 0)
    pl.semaphore_wait(barrier, count)

    for present, down in ((has_south, True), (has_north, False)):

        @pl.when(present)
        def _():
            info_copy(down).start()

    send_chunk(0, c_ref, 0)
    send_border(0)
    for k in range(1, chunks):
        send_chunk(0, c_ref, k)
    prepare(0)
    for present, down in ((has_north, True), (has_south, False)):

        @pl.when(present)
        def _():
            info_copy(down).wait_recv()

    prepare(1)
    prepare(2)
    overset(0, c_ref)

    def pulled(e, cols, at, here, acc):
        value = STEP_SIZE * acc
        w_ref[e, :, cols] = value
        hal_send[1, 0, e : e + 1, cols] = value[rows - 1 : rows]
        hal_send[1, 1, e : e + 1, cols] = value[0:1]

    for k in range(chunks):
        wait_chunk(0, c_ref, k)
        operator(0, k, pulled)
        if k == chunks - 1:
            pack_border(1, w_ref)
            send_border(1)
        send_chunk(1, w_ref, k)

    overset(1, w_ref)

    def final(e, cols, at, here, acc):
        out_ref[e, :, cols] = (
            v_ref[0, e, :, pl.ds(at + 128, BLK)] + here + (0.5 * STEP_SIZE) * acc
        )

    for k in range(chunks):
        wait_chunk(1, w_ref, k)
        operator(1, k, final)
    for present, down in ((has_south, True), (has_north, False)):

        @pl.when(present)
        def _():
            info_copy(down).wait_send()

    wait_sends(0, c_ref)
    wait_sends(1, w_ref)


def body(
    final_cotangent,
    diffusivity,
    theta_velocity,
    phi_velocity,
    radial_stencil,
    field_coupling,
    slot_targets,
    slot_donors,
    slot_weights,
    slot_counts,
):
    fields, _, rows, columns = final_cotangent.shape[1:]
    tiles, levels = lax.axis_size("hor"), lax.axis_size("rad")
    slots = slot_targets.shape[-1]
    nblk = columns // BLK
    chunks = 3 if nblk % 3 == 0 else 1
    window = -(-3 * (columns // tiles) // 128) * 128
    block = (fields, rows, columns)
    vmem = pl.BlockSpec(memory_space=pltpu.VMEM)
    smem = pl.BlockSpec(memory_space=pltpu.SMEM)
    hbm = pl.BlockSpec(memory_space=pltpu.HBM)
    dma = pltpu.SemaphoreType.DMA
    out = pl.pallas_call(
        functools.partial(kernel, tiles, levels, chunks),
        out_shape=jax.ShapeDtypeStruct(block, F32),
        in_specs=[hbm, hbm, hbm, hbm, smem, smem, hbm, hbm, hbm, smem],
        out_specs=vmem,
        scratch_shapes=[
            pltpu.VMEM(block, F32),
            pltpu.VMEM((3, rows, columns), F32),
            pltpu.VMEM((2, 1, 1, slots), jnp.int32),
            pltpu.VMEM((1, 1, slots), F32),
            pltpu.VMEM(block, F32),
            pltpu.VMEM((2, fields, rows, columns + 256), F32),
            pltpu.VMEM((2, 2, *block), F32),
            pltpu.VMEM((2, 2, fields, columns), F32),
            pltpu.VMEM((2, 2, fields, columns), F32),
            pltpu.VMEM((2, 1, 128), F32),
            pltpu.VMEM((2, tiles, 1, 128), F32),
            pltpu.VMEM((fields, columns + 384), F32),
            pltpu.VMEM((2, tiles, fields, window), F32),
            pltpu.VMEM((2, 2, fields, window), F32),
            pltpu.VMEM((2, fields, slots), F32),
            pltpu.VMEM((2, 2, fields, slots), F32),
            pltpu.VMEM((3, 3, 1, slots), F32),
            pltpu.VMEM((2 * window, 3 * slots), BF16),
            pltpu.VMEM((tiles, 3 * slots), BF16),
            pltpu.VMEM((1, 3 * slots), jnp.int32),
            pltpu.VMEM((3, 1, slots), jnp.int32),
            pltpu.VMEM((3, 2 * slots, BLK), BF16),
            pltpu.VMEM((nblk * fields * rows, 2 * slots), BF16),
            pltpu.VMEM((nblk * fields * rows, BLK), F32),
            pltpu.VMEM((nblk * fields * rows, BLK), F32),
            pltpu.VMEM((2, nblk * fields, BLK), F32),
            dma((7,)),
            dma((2, 2, chunks)),
            dma((2, 2, chunks)),
            dma((2, 2, chunks)),
            dma((2, 2, chunks)),
            dma((2,)),
            dma((2,)),
            dma((2,)),
            dma((2, 2)),
            dma((2, 2)),
            dma((2, 2)),
            dma((2,)),
            dma((2,)),
        ],
        compiler_params=pltpu.CompilerParams(
            collective_id=0, has_side_effects=True, vmem_limit_bytes=48 * 2**20
        ),
        cost_estimate=pl.CostEstimate(
            flops=8_000_000, bytes_accessed=1_500_000, transcendentals=0
        ),
    )(
        final_cotangent.reshape(block),
        diffusivity,
        theta_velocity,
        phi_velocity,
        radial_stencil,
        field_coupling,
        slot_targets,
        slot_donors,
        slot_weights,
        slot_counts,
    )
    return out.reshape(final_cotangent.shape)


def solution(mesh):
    return jax.shard_map(
        body,
        mesh=mesh,
        in_specs=(
            P("panel", None, "rad", "hor", None),
            P("panel", "rad", "hor", None),
            P("panel", "rad", "hor", None),
            P("panel", "rad", "hor", None),
            P(),
            P(),
            P("panel", "hor", None),
            P("panel", "hor", None),
            P("panel", "hor", None),
            P("panel", "hor"),
        ),
        out_specs=P("panel", None, "rad", "hor", None),
        check_vma=False,
    )
```

```python
import functools

import jax
import jax.numpy as jnp
from jax import lax
from jax.experimental import pallas as pl
from jax.experimental.pallas import tpu as pltpu
from jax.sharding import PartitionSpec as P

STEP_SIZE = 0.2
MESH = pl.DeviceIdType.MESH
F32 = jnp.float32
BF16 = jnp.bfloat16
BLK = 256


def split(x):
    hi = x.astype(BF16)
    lo = (x - hi.astype(F32)).astype(BF16)
    return hi, lo


def kernel(
    tiles,
    levels,
    chunks,
    c_hbm,
    kap_hbm,
    vt_hbm,
    vp_hbm,
    rs_ref,
    fc_ref,
    tgt_hbm,
    don_hbm,
    wt_hbm,
    cnt_ref,
    out_hbm,
    out_ref,
    c_ref,
    coef,
    ints,
    wts,
    w_ref,
    v_ref,
    rad_buf,
    hal_send,
    hal_recv,
    side_msg,
    side_buf,
    row_line,
    pieces,
    row_buf,
    val_send,
    val_recv,
    info,
    gather_rows,
    gather_sides,
    side_group,
    key_ref,
    lane_hot,
    spread,
    own_part,
    rad_part,
    hal_part,
    load_sem,
    store_sem,
    rad_ssem,
    rad_rsem,
    hal_ssem,
    hal_rsem,
    side_ssem,
    side_rsem,
    piece_ssem,
    piece_rsem,
    val_ssem,
    val_rsem,
    info_ssem,
    info_rsem,
):
    fields, rows, columns = c_ref.shape
    slots = key_ref.shape[2]
    window = row_buf.shape[3]
    per_tile = columns // tiles
    nblk = columns // BLK
    width = columns // chunks
    panel = lax.axis_index("panel")
    rad = lax.axis_index("rad")
    hor = lax.axis_index("hor")
    other = 1 - panel

    barrier = pltpu.get_barrier_semaphore()

    def greet(j, carry):
        pl.semaphore_signal(
            barrier, inc=1, device_id={"panel": other, "hor": j}, device_id_type=MESH
        )
        return carry

    lax.fori_loop(0, tiles, greet, 0)

    has_low, has_high = rad > 0, rad < levels - 1
    has_north, has_south = hor > 0, hor < tiles - 1

    def to_rad(step):
        return {"rad": rad + step}

    def to_hor(step):
        return {"hor": hor + step}

    around = (
        (has_low, to_rad(-1)),
        (has_high, to_rad(1)),
        (has_north, to_hor(-1)),
        (has_south, to_hor(1)),
    )
    for present, where in around:

        @pl.when(present)
        def _():
            pl.semaphore_signal(barrier, inc=1, device_id=where, device_id_type=MESH)

    loads = [
        pltpu.make_async_copy(src, dst, load_sem.at[k])
        for k, (src, dst) in enumerate(
            (
                (c_hbm, c_ref),
                (kap_hbm.at[0, 0], coef.at[0]),
                (vt_hbm.at[0, 0], coef.at[1]),
                (vp_hbm.at[0, 0], coef.at[2]),
                (tgt_hbm, ints.at[0]),
                (don_hbm, ints.at[1]),
                (wt_hbm, wts),
            )
        )
    ]
    for load in loads:
        load.start()

    row_ids = lax.broadcasted_iota(jnp.int32, (rows, BLK), 0)
    lane_ids = lax.broadcasted_iota(jnp.int32, (rows, BLK), 1)
    bad_row = ((row_ids == 0) & (hor == 0)) | ((row_ids == rows - 1) & (hor == tiles - 1))

    def side_mask(block):
        col = lane_ids + block * BLK
        return (col == 0) | (col == columns - 1)

    def remote(src, dst, send, recv, where):
        return pltpu.make_async_remote_copy(
            src_ref=src,
            dst_ref=dst,
            send_sem=send,
            recv_sem=recv,
            device_id=where,
            device_id_type=MESH,
        )

    def rad_copy(ph, src, up, k):
        slot = 0 if up else 1
        cols = pl.ds(k * width if isinstance(k, int) else pl.multiple_of(k * width, width), width)
        return remote(
            src.at[:, :, cols],
            rad_buf.at[ph, slot, :, :, cols],
            rad_ssem.at[ph, slot, k],
            rad_rsem.at[ph, slot, k],
            to_rad(1 if up else -1),
        )

    def hal_copy(ph, down, k):
        slot = 0 if down else 1
        cols = pl.ds(k * width if isinstance(k, int) else pl.multiple_of(k * width, width), width)
        return remote(
            hal_send.at[ph, slot, :, cols],
            hal_recv.at[ph, slot, :, cols],
            hal_ssem.at[ph, slot, k],
            hal_rsem.at[ph, slot, k],
            to_hor(1 if down else -1),
        )

    def val_copy(ph, up):
        slot = 0 if up else 1
        return remote(
            val_send.at[ph],
            val_recv.at[ph, slot],
            val_ssem.at[ph, slot],
            val_rsem.at[ph, slot],
            to_rad(1 if up else -1),
        )

    def info_copy(down):
        slot = 0 if down else 1
        return remote(
            info.at[0],
            info.at[1 + slot],
            info_ssem.at[slot],
            info_rsem.at[slot],
            to_hor(1 if down else -1),
        )

    def side_copy(ph, j):
        return remote(
            side_msg.at[ph],
            side_buf.at[ph, hor],
            side_ssem.at[ph],
            side_rsem.at[ph],
            {"panel": other, "hor": j},
        )

    def sides_all(ph):
        return remote(
            side_buf.at[ph], side_buf.at[ph], side_ssem.at[ph], side_rsem.at[ph], {"panel": other}
        )

    def piece_copy(ph, edge, j):
        return remote(
            pieces.at[ph, j],
            row_buf.at[ph, edge],
            piece_ssem.at[ph],
            piece_rsem.at[ph, edge],
            {"panel": other, "hor": j},
        )

    def pieces_all(ph):
        return remote(
            pieces.at[ph], pieces.at[ph], piece_ssem.at[ph], piece_rsem.at[ph, 0], {"panel": other}
        )

    def pack_border(ph, src):
        lanes = lax.broadcasted_iota(jnp.int32, (rows, 128), 1)
        both = jnp.zeros((rows, 128), F32)
        for f in range(fields):
            first = src[f, :, 0:1]
            last = src[f, :, columns - 1 : columns]
            both = jnp.where(lanes == f, first, both)
            both = jnp.where(lanes == fields + f, last, both)
        turned = pltpu.roll(both, 0, 1, stride=2 * fields, stride_axis=0)
        side_msg[ph] = jnp.sum(turned, axis=0, keepdims=True)

        for edge, row, here in ((0, 0, hor == 0), (1, rows - 1, hor == tiles - 1)):

            @pl.when(here)
            def _():
                for f in range(fields):
                    row_line[f : f + 1, 128 : 128 + columns] = src[f, row : row + 1, :]
                row_line[:, 0:128] = jnp.zeros((fields, 128), F32)
                row_line[:, columns + 128 : columns + 384] = jnp.zeros((fields, 256), F32)
                for j in range(tiles):
                    base, off = divmod(128 + per_tile * (j - 1), 128)
                    one = row_line[:, base * 128 : base * 128 + window + 128]
                    if off:
                        one = pltpu.roll(one, window + 128 - off, 1)
                    pieces[ph, j] = one[:, 0:window]

    def send_border(ph):
        for edge, here in ((0, hor == 0), (1, hor == tiles - 1)):

            @pl.when(here)
            def _():
                def row(j, carry):
                    piece_copy(ph, edge, j).start()
                    return carry

                lax.fori_loop(0, tiles, row, 0)

        def one(j, carry):
            side_copy(ph, j).start()
            return carry

        lax.fori_loop(0, tiles, one, 0)

    def send_chunk(ph, src, k):
        for present, copy in (
            (has_high, lambda: rad_copy(ph, src, True, k)),
            (has_low, lambda: rad_copy(ph, src, False, k)),
            (has_south, lambda: hal_copy(ph, True, k)),
            (has_north, lambda: hal_copy(ph, False, k)),
        ):

            @pl.when(present)
            def _():
                copy().start()

    def sent_chunk(ph, src, k):
        for present, copy in (
            (has_high, lambda: rad_copy(ph, src, True, k)),
            (has_low, lambda: rad_copy(ph, src, False, k)),
            (has_south, lambda: hal_copy(ph, True, k)),
            (has_north, lambda: hal_copy(ph, False, k)),
        ):

            @pl.when(present)
            def _():
                copy().wait_send()

    class Stream:
        def __init__(self, ph, src):
            self.ph, self.src, self.begun, self.ended = ph, src, 0, 0
            self.begin()
            self.begin()

        def begin(self):
            if self.begun < chunks:
                send_chunk(self.ph, self.src, self.begun)
                self.begun += 1

        def step(self):
            if self.ended < self.begun:
                sent_chunk(self.ph, self.src, self.ended)
                self.ended += 1
                self.begin()

        def finish(self):
            while self.ended < self.begun:
                self.step()

    def wait_chunk(ph, src, k):
        for present, copy in (
            (has_low, lambda: rad_copy(ph, src, True, k)),
            (has_high, lambda: rad_copy(ph, src, False, k)),
            (has_north, lambda: hal_copy(ph, True, k)),
            (has_south, lambda: hal_copy(ph, False, k)),
        ):

            @pl.when(present)
            def _():
                copy().wait_recv()

    def prepare(which):
        tgt = info[which, 0].astype(jnp.int32)
        don = info[which, 1].astype(jnp.int32)
        at = pl.ds(which * slots, slots)
        first = tgt - per_tile * (hor - 1)
        second = first - columns + window
        entry = jnp.where(tgt < columns, first, jnp.where(tgt < 2 * columns, second, -1))
        ids = lax.broadcasted_iota(jnp.int32, (2 * window, slots), 0)
        gather_rows[:, at] = jnp.where(ids == entry, F32(1), F32(0)).astype(BF16)
        place = tgt - 2 * columns
        far = jnp.where(place >= tiles * rows, 1, 0)
        line = place - far * (tiles * rows)
        tile = jnp.where(place >= 0, line >> 3, -1)
        hids = lax.broadcasted_iota(jnp.int32, (tiles, slots), 0)
        gather_sides[:, at] = jnp.where(hids == tile, F32(1), F32(0)).astype(BF16)
        side_group[:, at] = 2 * (line & 7) + far
        local = jnp.zeros_like(don)
        for m in range(1, rows):
            local = local + jnp.where(don >= m * columns, 1, 0)
        col = don - local * columns
        block = col >> 8
        if which == 0:
            key_ref[which] = block * rows + local
        elif which == 1:
            key_ref[which] = jnp.where(local == rows - 1, block, -1)
        else:
            key_ref[which] = jnp.where(local == 0, block, -1)
        lane = jnp.broadcast_to((col & (BLK - 1)).astype(F32), (8, slots)).T[:, 0:1]
        ids = lax.broadcasted_iota(jnp.int32, (slots, BLK), 1).astype(F32)
        hot = jnp.where(ids == lane, F32(1), F32(0)).astype(BF16)
        lane_hot[which, 0:slots, :] = hot
        lane_hot[which, slots : 2 * slots, :] = hot

    def gather(ph):
        table = jnp.concatenate([row_buf[ph, 0], row_buf[ph, 1]], axis=1)
        hi, lo = split(table)
        got = jnp.dot(
            jnp.concatenate([hi, lo], axis=0), gather_rows[...], preferred_element_type=F32
        )
        total = got[0:fields] + got[fields : 2 * fields]
        turned = side_buf[ph, :, 0, :].T
        hi, lo = split(turned)
        got = jnp.dot(
            jnp.concatenate([hi, lo], axis=0), gather_sides[...], preferred_element_type=F32
        )
        got = got[0:128] + got[128:256]
        group = side_group[...]
        for g in range(2 * rows):
            part = got[g * fields : (g + 1) * fields]
            total = total + jnp.where(group == g, part, F32(0.0))
        return [
            total[:, n * slots : (n + 1) * slots] * info[n, 2] for n in range(3)
        ]

    def scatter(values, into):
        hi, lo = split(values)
        hi, lo = hi.astype(F32), lo.astype(F32)
        key = key_ref[0]
        own = lax.broadcasted_iota(jnp.int32, (rows, slots), 0)

        def one(block, carry):
            hit = key == own + block * rows
            at = pl.multiple_of(block * (fields * rows), fields * rows)
            for part, x in ((0, hi), (1, lo)):
                picked = [jnp.where(hit, x[f : f + 1], F32(0.0)) for f in range(fields)]
                spread[pl.ds(at, fields * rows), part * slots : (part + 1) * slots] = (
                    jnp.concatenate(picked, axis=0).astype(BF16)
                )
            return carry

        lax.fori_loop(0, nblk, one, 0)
        into[...] = jnp.dot(spread[...], lane_hot[0], preferred_element_type=F32)

    def scatter_row(which, values):
        hi, lo = split(values)
        key = key_ref[which]
        both = []
        for x in (hi.astype(F32), lo.astype(F32)):
            picked = [jnp.where(key == b, x, F32(0.0)) for b in range(nblk)]
            both.append(jnp.concatenate(picked, axis=0).astype(BF16))
        hal_part[which - 1] = jnp.dot(
            jnp.concatenate(both, axis=1), lane_hot[which], preferred_element_type=F32
        )

    def coefficients(f):
        low = rs_ref[1, jnp.maximum(rad - 1, 0), f]
        high = rs_ref[2, jnp.minimum(rad + 1, levels - 1), f]
        low = jnp.where(has_low, low, F32(0.0))
        high = jnp.where(has_high, high, F32(0.0))
        return low, high

    def overset(ph, src, stream):
        sides_all(ph).wait_recv()
        piece_copy(ph, 0, 0).wait_recv()
        piece_copy(ph, 1, 0).wait_recv()
        values, from_north, from_south = gather(ph)
        val_send[ph] = values

        @pl.when(has_high)
        def _():
            val_copy(ph, True).start()

        @pl.when(has_low)
        def _():
            val_copy(ph, False).start()

        stream.step()
        scatter(values, own_part)
        stream.step()

        def one(block, carry):
            at = pl.multiple_of(block * BLK, BLK)
            border = bad_row | side_mask(block)
            for f in range(fields):
                start = pl.multiple_of(block * (fields * rows) + f * rows, rows)
                x = jnp.where(border, F32(0.0), src[f, :, pl.ds(at, BLK)])
                v_ref[ph, f, :, pl.ds(at + 128, BLK)] = x + own_part[pl.ds(start, rows), :]
            return carry

        lax.fori_loop(0, nblk, one, 0)
        scatter_row(1, from_north)
        scatter_row(2, from_south)
        stream.step()

        @pl.when(has_low)
        def _():
            val_copy(ph, True).wait_recv()

        @pl.when(has_high)
        def _():
            val_copy(ph, False).wait_recv()

        mixed = []
        for f in range(fields):
            low, high = coefficients(f)
            mixed.append(
                low * val_recv[ph, 0, f : f + 1, :] + high * val_recv[ph, 1, f : f + 1, :]
            )
        scatter(jnp.concatenate(mixed, axis=0), rad_part)

    def wait_sends(ph):
        for present, copy in (
            (has_high, lambda: val_copy(ph, True)),
            (has_low, lambda: val_copy(ph, False)),
            ((hor == 0) | (hor == tiles - 1), lambda: pieces_all(ph)),
        ):

            @pl.when(present)
            def _():
                copy().wait_send()

        sides_all(ph).wait_send()

    def operator(ph, k, finish):
        def one(block, carry):
            at = pl.multiple_of(block * BLK, BLK)
            cols = pl.ds(at, BLK)
            kap = coef[0, :, cols]
            vt = coef[1, :, cols]
            vp = coef[2, :, cols]
            north, south = kap + vt, kap - vt
            east, west = kap + vp, kap - vp
            center = 4.0 * kap
            sides = side_mask(block)
            border = bad_row | sides
            here, total = [], []
            for f in range(fields):
                wide = v_ref[ph, f, :, pl.ds(at, BLK + 256)]
                cur = wide[:, 128 : 128 + BLK]
                before = pltpu.roll(wide, 1, 1)[:, 128 : 128 + BLK]
                after = pltpu.roll(wide, BLK + 255, 1)[:, 128 : 128 + BLK]
                line = block * fields + f
                edge = []
                for n in range(2):
                    raw = jnp.where(sides[0:1], F32(0.0), hal_recv[ph, n, f : f + 1, cols])
                    edge.append(raw + hal_part[n, pl.ds(line, 1), :])
                below = jnp.where(row_ids == 0, edge[0], pltpu.roll(cur, 1, 0))
                above = jnp.where(row_ids == rows - 1, edge[1], pltpu.roll(cur, rows - 1, 0))
                low, high = coefficients(f)
                start = pl.multiple_of(block * (fields * rows) + f * rows, rows)
                mixed = low * rad_buf[ph, 0, f, :, cols] + high * rad_buf[ph, 1, f, :, cols]
                acc = jnp.where(border, F32(0.0), mixed) + rad_part[pl.ds(start, rows), :]
                acc = acc + south * below + north * above + west * before + east * after
                acc = acc - center * cur + rs_ref[0, rad, f] * cur
                here.append(cur)
                total.append(acc)
            for e in range(fields):
                acc = total[e]
                for f in range(fields):
                    acc = acc + fc_ref[rad, f, e] * here[f]
                finish(e, cols, at, here[e], acc)
            return carry

        return one(k, 0)

    loads[0].wait()
    pack_border(0, c_ref)

    count = tiles
    for present, _ in around:
        count = count + jnp.where(present, 1, 0)
    pl.semaphore_wait(barrier, count)
    send_border(0)

    for load in loads[1:]:
        load.wait()
    slot_ids = lax.broadcasted_iota(jnp.int32, (1, slots), 1)
    info[0, 0] = ints[0, 0].astype(F32)
    info[0, 1] = ints[1, 0].astype(F32)
    info[0, 2] = jnp.where(slot_ids < cnt_ref[0, 0], wts[0], F32(0.0))
    for present, down in ((has_south, True), (has_north, False)):

        @pl.when(present)
        def _():
            info_copy(down).start()

    for f in range(fields):
        hal_send[0, 0, f : f + 1, :] = c_ref[f, rows - 1 : rows, :]
        hal_send[0, 1, f : f + 1, :] = c_ref[f, 0:1, :]
    stream = Stream(0, c_ref)

    zero_block = jnp.zeros((2, fields, rows, 128), F32)
    v_ref[:, :, :, 0:128] = zero_block
    v_ref[:, :, :, columns + 128 : columns + 256] = zero_block
    for present, slot in ((has_low, 0), (has_high, 1)):

        @pl.when(jnp.logical_not(present))
        def _():
            for ph in range(2):
                rad_buf[ph, slot] = jnp.zeros(rad_buf.shape[2:], F32)
                val_recv[ph, slot] = jnp.zeros(val_recv.shape[2:], F32)

    for present, slot in ((has_north, 0), (has_south, 1)):

        @pl.when(jnp.logical_not(present))
        def _():
            info[1 + slot] = jnp.zeros(info.shape[1:], F32)
            for ph in range(2):
                hal_recv[ph, slot] = jnp.zeros(hal_recv.shape[2:], F32)

    prepare(0)
    stream.step()
    stream.step()
    stream.step()
    for present, down in ((has_north, True), (has_south, False)):

        @pl.when(present)
        def _():
            info_copy(down).wait_recv()

    prepare(1)
    prepare(2)
    stream.step()
    overset(0, c_ref, stream)
    stream.finish()

    def pulled(e, cols, at, here, acc):
        value = STEP_SIZE * acc
        w_ref[e, :, cols] = value
        hal_send[1, 0, e : e + 1, cols] = value[rows - 1 : rows]
        hal_send[1, 1, e : e + 1, cols] = value[0:1]

    def first(k, carry):
        wait_chunk(0, c_ref, k)
        operator(0, k, pulled)
        return carry

    lax.fori_loop(0, chunks, first, 0)
    pack_border(1, w_ref)
    send_border(1)
    stream = Stream(1, w_ref)
    for _ in range(3):
        stream.step()
    overset(1, w_ref, stream)
    stream.finish()

    def final(e, cols, at, here, acc):
        out_ref[e, :, cols] = (
            v_ref[0, e, :, pl.ds(at + 128, BLK)] + here + (0.5 * STEP_SIZE) * acc
        )

    def second(k, carry):
        wait_chunk(1, w_ref, k)
        operator(1, k, final)
        cols = pl.ds(pl.multiple_of(k * width, width), width)
        pltpu.make_async_copy(
            out_ref.at[:, :, cols], out_hbm.at[:, :, cols], store_sem
        ).start()
        return carry

    lax.fori_loop(0, chunks, second, 0)
    for present, down in ((has_south, True), (has_north, False)):

        @pl.when(present)
        def _():
            info_copy(down).wait_send()

    wait_sends(0)
    wait_sends(1)
    pltpu.make_async_copy(out_ref, out_hbm, store_sem).wait()


def body(
    final_cotangent,
    diffusivity,
    theta_velocity,
    phi_velocity,
    radial_stencil,
    field_coupling,
    slot_targets,
    slot_donors,
    slot_weights,
    slot_counts,
):
    fields, _, rows, columns = final_cotangent.shape[1:]
    tiles, levels = lax.axis_size("hor"), lax.axis_size("rad")
    slots = slot_targets.shape[-1]
    nblk = columns // BLK
    chunks = nblk
    window = -(-3 * (columns // tiles) // 128) * 128
    block = (fields, rows, columns)
    smem = pl.BlockSpec(memory_space=pltpu.SMEM)
    hbm = pl.BlockSpec(memory_space=pltpu.HBM)
    dma = pltpu.SemaphoreType.DMA
    out = pl.pallas_call(
        functools.partial(kernel, tiles, levels, chunks),
        out_shape=jax.ShapeDtypeStruct(block, F32),
        in_specs=[hbm, hbm, hbm, hbm, smem, smem, hbm, hbm, hbm, smem],
        out_specs=hbm,
        scratch_shapes=[
            pltpu.VMEM(block, F32),
            pltpu.VMEM(block, F32),
            pltpu.VMEM((3, rows, columns), F32),
            pltpu.VMEM((2, 1, 1, slots), jnp.int32),
            pltpu.VMEM((1, 1, slots), F32),
            pltpu.VMEM(block, F32),
            pltpu.VMEM((2, fields, rows, columns + 256), F32),
            pltpu.VMEM((2, 2, *block), F32),
            pltpu.VMEM((2, 2, fields, columns), F32),
            pltpu.VMEM((2, 2, fields, columns), F32),
            pltpu.VMEM((2, 1, 128), F32),
            pltpu.VMEM((2, tiles, 1, 128), F32),
            pltpu.VMEM((fields, columns + 384), F32),
            pltpu.VMEM((2, tiles, fields, window), F32),
            pltpu.VMEM((2, 2, fields, window), F32),
            pltpu.VMEM((2, fields, slots), F32),
            pltpu.VMEM((2, 2, fields, slots), F32),
            pltpu.VMEM((3, 3, 1, slots), F32),
            pltpu.VMEM((2 * window, 3 * slots), BF16),
            pltpu.VMEM((tiles, 3 * slots), BF16),
            pltpu.VMEM((1, 3 * slots), jnp.int32),
            pltpu.VMEM((3, 1, slots), jnp.int32),
            pltpu.VMEM((3, 2 * slots, BLK), BF16),
            pltpu.VMEM((nblk * fields * rows, 2 * slots), BF16),
            pltpu.VMEM((nblk * fields * rows, BLK), F32),
            pltpu.VMEM((nblk * fields * rows, BLK), F32),
            pltpu.VMEM((2, nblk * fields, BLK), F32),
            dma((7,)),
            dma(()),
            dma((2, 2, chunks)),
            dma((2, 2, chunks)),
            dma((2, 2, chunks)),
            dma((2, 2, chunks)),
            dma((2,)),
            dma((2,)),
            dma((2,)),
            dma((2, 2)),
            dma((2, 2)),
            dma((2, 2)),
            dma((2,)),
            dma((2,)),
        ],
        compiler_params=pltpu.CompilerParams(
            collective_id=0, has_side_effects=True, vmem_limit_bytes=60 * 2**20
        ),
        cost_estimate=pl.CostEstimate(
            flops=8_000_000, bytes_accessed=1_500_000, transcendentals=0
        ),
    )(
        final_cotangent.reshape(block),
        diffusivity,
        theta_velocity,
        phi_velocity,
        jnp.swapaxes(radial_stencil, 1, 2),
        field_coupling,
        slot_targets,
        slot_donors,
        slot_weights,
        slot_counts,
    )
    return out.reshape(final_cotangent.shape)


def solution(mesh):
    return jax.shard_map(
        body,
        mesh=mesh,
        in_specs=(
            P("panel", None, "rad", "hor", None),
            P("panel", "rad", "hor", None),
            P("panel", "rad", "hor", None),
            P("panel", "rad", "hor", None),
            P(),
            P(),
            P("panel", "hor", None),
            P("panel", "hor", None),
            P("panel", "hor", None),
            P("panel", "hor"),
        ),
        out_specs=P("panel", None, "rad", "hor", None),
        check_vma=False,
    )
```

```python
import functools

import jax
import jax.numpy as jnp
from jax import lax
from jax.experimental import pallas as pl
from jax.experimental.pallas import tpu as pltpu
from jax.sharding import PartitionSpec as P

STEP_SIZE = 0.2
MESH = pl.DeviceIdType.MESH
F32 = jnp.float32
BF16 = jnp.bfloat16
BLK = 256
DEPTH = 2


def split(x):
    hi = x.astype(BF16)
    lo = (x - hi.astype(F32)).astype(BF16)
    return hi, lo


def kernel(
    tiles,
    levels,
    chunks,
    c_hbm,
    kap_hbm,
    vt_hbm,
    vp_hbm,
    rs_ref,
    fc_ref,
    tgt_hbm,
    don_hbm,
    wt_hbm,
    cnt_ref,
    out_hbm,
    out_ref,
    c_ref,
    coef,
    ints,
    wts,
    w_ref,
    v_ref,
    rad_buf,
    hal_send,
    hal_recv,
    side_msg,
    side_buf,
    row_line,
    pieces,
    row_buf,
    val_send,
    val_recv,
    info,
    gather_rows,
    gather_sides,
    side_group,
    key_ref,
    lane_hot,
    spread,
    own_part,
    rad_part,
    hal_part,
    load_sem,
    store_sem,
    rad_ssem,
    rad_rsem,
    hal_ssem,
    hal_rsem,
    side_ssem,
    side_rsem,
    piece_ssem,
    piece_rsem,
    val_ssem,
    val_rsem,
    info_ssem,
    info_rsem,
):
    fields, rows, columns = c_ref.shape
    slots = key_ref.shape[2]
    window = row_buf.shape[3]
    per_tile = columns // tiles
    nblk = columns // BLK
    width = columns // chunks
    panel = lax.axis_index("panel")
    rad = lax.axis_index("rad")
    hor = lax.axis_index("hor")
    other = 1 - panel

    barrier = pltpu.get_barrier_semaphore()

    def greet(j, carry):
        pl.semaphore_signal(
            barrier, inc=1, device_id={"panel": other, "hor": j}, device_id_type=MESH
        )
        return carry

    lax.fori_loop(0, tiles, greet, 0)

    has_low, has_high = rad > 0, rad < levels - 1
    has_north, has_south = hor > 0, hor < tiles - 1

    def to_rad(step):
        return {"rad": rad + step}

    def to_hor(step):
        return {"hor": hor + step}

    around = (
        (has_low, to_rad(-1)),
        (has_high, to_rad(1)),
        (has_north, to_hor(-1)),
        (has_south, to_hor(1)),
    )
    for present, where in around:

        @pl.when(present)
        def _():
            pl.semaphore_signal(barrier, inc=1, device_id=where, device_id_type=MESH)

    loads = [
        pltpu.make_async_copy(src, dst, load_sem.at[k])
        for k, (src, dst) in enumerate(
            (
                (c_hbm, c_ref),
                (kap_hbm.at[0, 0], coef.at[0]),
                (vt_hbm.at[0, 0], coef.at[1]),
                (vp_hbm.at[0, 0], coef.at[2]),
                (tgt_hbm, ints.at[0]),
                (don_hbm, ints.at[1]),
                (wt_hbm, wts),
            )
        )
    ]
    for load in loads:
        load.start()

    row_ids = lax.broadcasted_iota(jnp.int32, (rows, BLK), 0)
    lane_ids = lax.broadcasted_iota(jnp.int32, (rows, BLK), 1)
    bad_row = ((row_ids == 0) & (hor == 0)) | ((row_ids == rows - 1) & (hor == tiles - 1))

    def side_mask(block):
        col = lane_ids + block * BLK
        return (col == 0) | (col == columns - 1)

    def remote(src, dst, send, recv, where):
        return pltpu.make_async_remote_copy(
            src_ref=src,
            dst_ref=dst,
            send_sem=send,
            recv_sem=recv,
            device_id=where,
            device_id_type=MESH,
        )

    def rad_copy(ph, src, up, k):
        slot = 0 if up else 1
        cols = pl.ds(k * width if isinstance(k, int) else pl.multiple_of(k * width, width), width)
        return remote(
            src.at[:, :, cols],
            rad_buf.at[ph, slot, :, :, cols],
            rad_ssem.at[ph, slot, k],
            rad_rsem.at[ph, slot, k],
            to_rad(1 if up else -1),
        )

    def hal_copy(ph, down, k):
        slot = 0 if down else 1
        cols = pl.ds(k * width if isinstance(k, int) else pl.multiple_of(k * width, width), width)
        return remote(
            hal_send.at[ph, slot, :, cols],
            hal_recv.at[ph, slot, :, cols],
            hal_ssem.at[ph, slot, k],
            hal_rsem.at[ph, slot, k],
            to_hor(1 if down else -1),
        )

    def val_copy(ph, up):
        slot = 0 if up else 1
        return remote(
            val_send.at[ph],
            val_recv.at[ph, slot],
            val_ssem.at[ph, slot],
            val_rsem.at[ph, slot],
            to_rad(1 if up else -1),
        )

    def info_copy(down):
        slot = 0 if down else 1
        return remote(
            info.at[0],
            info.at[1 + slot],
            info_ssem.at[slot],
            info_rsem.at[slot],
            to_hor(1 if down else -1),
        )

    def side_copy(ph, j):
        return remote(
            side_msg.at[ph],
            side_buf.at[ph, hor],
            side_ssem.at[ph],
            side_rsem.at[ph],
            {"panel": other, "hor": j},
        )

    def sides_all(ph):
        return remote(
            side_buf.at[ph], side_buf.at[ph], side_ssem.at[ph], side_rsem.at[ph], {"panel": other}
        )

    def piece_copy(ph, edge, j):
        return remote(
            pieces.at[ph, j],
            row_buf.at[ph, edge],
            piece_ssem.at[ph],
            piece_rsem.at[ph, edge],
            {"panel": other, "hor": j},
        )

    def pieces_all(ph):
        return remote(
            pieces.at[ph], pieces.at[ph], piece_ssem.at[ph], piece_rsem.at[ph, 0], {"panel": other}
        )

    def pack_border(ph, src):
        lanes = lax.broadcasted_iota(jnp.int32, (rows, 128), 1)
        both = jnp.zeros((rows, 128), F32)
        for f in range(fields):
            first = src[f, :, 0:1]
            last = src[f, :, columns - 1 : columns]
            both = jnp.where(lanes == f, first, both)
            both = jnp.where(lanes == fields + f, last, both)
        turned = pltpu.roll(both, 0, 1, stride=2 * fields, stride_axis=0)
        side_msg[ph] = jnp.sum(turned, axis=0, keepdims=True)

        for edge, row, here in ((0, 0, hor == 0), (1, rows - 1, hor == tiles - 1)):

            @pl.when(here)
            def _():
                for f in range(fields):
                    row_line[f : f + 1, 128 : 128 + columns] = src[f, row : row + 1, :]
                row_line[:, 0:128] = jnp.zeros((fields, 128), F32)
                row_line[:, columns + 128 : columns + 384] = jnp.zeros((fields, 256), F32)
                for j in range(tiles):
                    base, off = divmod(128 + per_tile * (j - 1), 128)
                    one = row_line[:, base * 128 : base * 128 + window + 128]
                    if off:
                        one = pltpu.roll(one, window + 128 - off, 1)
                    pieces[ph, j] = one[:, 0:window]

    def send_border(ph):
        for edge, here in ((0, hor == 0), (1, hor == tiles - 1)):

            @pl.when(here)
            def _():
                def row(j, carry):
                    piece_copy(ph, edge, j).start()
                    return carry

                lax.fori_loop(0, tiles, row, 0)

        def one(j, carry):
            side_copy(ph, j).start()
            return carry

        lax.fori_loop(0, tiles, one, 0)

    def send_chunk(ph, src, k):
        for present, copy in (
            (has_high, lambda: rad_copy(ph, src, True, k)),
            (has_low, lambda: rad_copy(ph, src, False, k)),
            (has_south, lambda: hal_copy(ph, True, k)),
            (has_north, lambda: hal_copy(ph, False, k)),
        ):

            @pl.when(present)
            def _():
                copy().start()

    def sent_chunk(ph, src, k):
        for present, copy in (
            (has_high, lambda: rad_copy(ph, src, True, k)),
            (has_low, lambda: rad_copy(ph, src, False, k)),
            (has_south, lambda: hal_copy(ph, True, k)),
            (has_north, lambda: hal_copy(ph, False, k)),
        ):

            @pl.when(present)
            def _():
                copy().wait_send()

    class Stream:
        def __init__(self, ph, src):
            self.ph, self.src, self.begun, self.ended = ph, src, 0, 0
            for _ in range(DEPTH):
                self.begin()

        def begin(self):
            if self.begun < chunks:
                send_chunk(self.ph, self.src, self.begun)
                self.begun += 1

        def step(self):
            if self.ended < self.begun:
                sent_chunk(self.ph, self.src, self.ended)
                self.ended += 1
                self.begin()

        def finish(self):
            while self.ended < self.begun:
                self.step()

    def wait_chunk(ph, src, k):
        for present, copy in (
            (has_low, lambda: rad_copy(ph, src, True, k)),
            (has_high, lambda: rad_copy(ph, src, False, k)),
            (has_north, lambda: hal_copy(ph, True, k)),
            (has_south, lambda: hal_copy(ph, False, k)),
        ):

            @pl.when(present)
            def _():
                copy().wait_recv()

    def prepare(which):
        tgt = info[which, 0].astype(jnp.int32)
        don = info[which, 1].astype(jnp.int32)
        at = pl.ds(which * slots, slots)
        first = tgt - per_tile * (hor - 1)
        second = first - columns + window
        entry = jnp.where(tgt < columns, first, jnp.where(tgt < 2 * columns, second, -1))
        ids = lax.broadcasted_iota(jnp.int32, (2 * window, slots), 0)
        gather_rows[:, at] = jnp.where(ids == entry, F32(1), F32(0)).astype(BF16)
        place = tgt - 2 * columns
        far = jnp.where(place >= tiles * rows, 1, 0)
        line = place - far * (tiles * rows)
        tile = jnp.where(place >= 0, line >> 3, -1)
        hids = lax.broadcasted_iota(jnp.int32, (tiles, slots), 0)
        gather_sides[:, at] = jnp.where(hids == tile, F32(1), F32(0)).astype(BF16)
        side_group[:, at] = 2 * (line & 7) + far
        local = jnp.zeros_like(don)
        for m in range(1, rows):
            local = local + jnp.where(don >= m * columns, 1, 0)
        col = don - local * columns
        block = col >> 8
        if which == 0:
            key_ref[which] = block * rows + local
        elif which == 1:
            key_ref[which] = jnp.where(local == rows - 1, block, -1)
        else:
            key_ref[which] = jnp.where(local == 0, block, -1)
        lane = jnp.broadcast_to((col & (BLK - 1)).astype(F32), (8, slots)).T[:, 0:1]
        ids = lax.broadcasted_iota(jnp.int32, (slots, BLK), 1).astype(F32)
        hot = jnp.where(ids == lane, F32(1), F32(0)).astype(BF16)
        lane_hot[which, 0:slots, :] = hot
        lane_hot[which, slots : 2 * slots, :] = hot

    def gather(ph):
        table = jnp.concatenate([row_buf[ph, 0], row_buf[ph, 1]], axis=1)
        hi, lo = split(table)
        got = jnp.dot(
            jnp.concatenate([hi, lo], axis=0), gather_rows[...], preferred_element_type=F32
        )
        total = got[0:fields] + got[fields : 2 * fields]
        turned = side_buf[ph, :, 0, :].T
        hi, lo = split(turned)
        got = jnp.dot(
            jnp.concatenate([hi, lo], axis=0), gather_sides[...], preferred_element_type=F32
        )
        got = got[0:128] + got[128:256]
        group = side_group[...]
        for g in range(2 * rows):
            part = got[g * fields : (g + 1) * fields]
            total = total + jnp.where(group == g, part, F32(0.0))
        return [
            total[:, n * slots : (n + 1) * slots] * info[n, 2] for n in range(3)
        ]

    def scatter(values, into):
        hi, lo = split(values)
        hi, lo = hi.astype(F32), lo.astype(F32)
        key = key_ref[0]
        own = lax.broadcasted_iota(jnp.int32, (rows, slots), 0)

        def one(block, carry):
            hit = key == own + block * rows
            at = pl.multiple_of(block * (fields * rows), fields * rows)
            for part, x in ((0, hi), (1, lo)):
                picked = [jnp.where(hit, x[f : f + 1], F32(0.0)) for f in range(fields)]
                spread[pl.ds(at, fields * rows), part * slots : (part + 1) * slots] = (
                    jnp.concatenate(picked, axis=0).astype(BF16)
                )
            return carry

        lax.fori_loop(0, nblk, one, 0)
        into[...] = jnp.dot(spread[...], lane_hot[0], preferred_element_type=F32)

    def scatter_row(which, values):
        hi, lo = split(values)
        key = key_ref[which]
        both = []
        for x in (hi.astype(F32), lo.astype(F32)):
            picked = [jnp.where(key == b, x, F32(0.0)) for b in range(nblk)]
            both.append(jnp.concatenate(picked, axis=0).astype(BF16))
        hal_part[which - 1] = jnp.dot(
            jnp.concatenate(both, axis=1), lane_hot[which], preferred_element_type=F32
        )

    def coefficients(f):
        low = rs_ref[1, jnp.maximum(rad - 1, 0), f]
        high = rs_ref[2, jnp.minimum(rad + 1, levels - 1), f]
        low = jnp.where(has_low, low, F32(0.0))
        high = jnp.where(has_high, high, F32(0.0))
        return low, high

    def overset(ph, src, stream):
        sides_all(ph).wait_recv()
        piece_copy(ph, 0, 0).wait_recv()
        piece_copy(ph, 1, 0).wait_recv()
        values, from_north, from_south = gather(ph)
        val_send[ph] = values

        @pl.when(has_high)
        def _():
            val_copy(ph, True).start()

        @pl.when(has_low)
        def _():
            val_copy(ph, False).start()

        stream.step()
        scatter(values, own_part)
        stream.step()

        def one(block, carry):
            at = pl.multiple_of(block * BLK, BLK)
            border = bad_row | side_mask(block)
            for f in range(fields):
                start = pl.multiple_of(block * (fields * rows) + f * rows, rows)
                x = jnp.where(border, F32(0.0), src[f, :, pl.ds(at, BLK)])
                v_ref[ph, f, :, pl.ds(at + 128, BLK)] = x + own_part[pl.ds(start, rows), :]
            return carry

        lax.fori_loop(0, nblk, one, 0)
        scatter_row(1, from_north)
        scatter_row(2, from_south)
        stream.step()

        @pl.when(has_low)
        def _():
            val_copy(ph, True).wait_recv()

        @pl.when(has_high)
        def _():
            val_copy(ph, False).wait_recv()

        mixed = []
        for f in range(fields):
            low, high = coefficients(f)
            mixed.append(
                low * val_recv[ph, 0, f : f + 1, :] + high * val_recv[ph, 1, f : f + 1, :]
            )
        scatter(jnp.concatenate(mixed, axis=0), rad_part)

    def wait_sends(ph):
        for present, copy in (
            (has_high, lambda: val_copy(ph, True)),
            (has_low, lambda: val_copy(ph, False)),
            ((hor == 0) | (hor == tiles - 1), lambda: pieces_all(ph)),
        ):

            @pl.when(present)
            def _():
                copy().wait_send()

        sides_all(ph).wait_send()

    def operator(ph, k, finish):
        def one(block, carry):
            at = pl.multiple_of(block * BLK, BLK)
            cols = pl.ds(at, BLK)
            kap = coef[0, :, cols]
            vt = coef[1, :, cols]
            vp = coef[2, :, cols]
            north, south = kap + vt, kap - vt
            east, west = kap + vp, kap - vp
            center = 4.0 * kap
            sides = side_mask(block)
            border = bad_row | sides
            here, total = [], []
            for f in range(fields):
                wide = v_ref[ph, f, :, pl.ds(at, BLK + 256)]
                cur = wide[:, 128 : 128 + BLK]
                before = pltpu.roll(wide, 1, 1)[:, 128 : 128 + BLK]
                after = pltpu.roll(wide, BLK + 255, 1)[:, 128 : 128 + BLK]
                line = block * fields + f
                edge = []
                for n in range(2):
                    raw = jnp.where(sides[0:1], F32(0.0), hal_recv[ph, n, f : f + 1, cols])
                    edge.append(raw + hal_part[n, pl.ds(line, 1), :])
                below = jnp.where(row_ids == 0, edge[0], pltpu.roll(cur, 1, 0))
                above = jnp.where(row_ids == rows - 1, edge[1], pltpu.roll(cur, rows - 1, 0))
                low, high = coefficients(f)
                start = pl.multiple_of(block * (fields * rows) + f * rows, rows)
                mixed = low * rad_buf[ph, 0, f, :, cols] + high * rad_buf[ph, 1, f, :, cols]
                acc = jnp.where(border, F32(0.0), mixed) + rad_part[pl.ds(start, rows), :]
                acc = acc + south * below + north * above + west * before + east * after
                acc = acc - center * cur + rs_ref[0, rad, f] * cur
                here.append(cur)
                total.append(acc)
            for e in range(fields):
                acc = total[e]
                for f in range(fields):
                    acc = acc + fc_ref[rad, f, e] * here[f]
                finish(e, cols, at, here[e], acc)
            return carry

        return one(k, 0)

    loads[0].wait()
    pack_border(0, c_ref)

    count = tiles
    for present, _ in around:
        count = count + jnp.where(present, 1, 0)
    pl.semaphore_wait(barrier, count)
    send_border(0)

    for load in loads[1:]:
        load.wait()
    slot_ids = lax.broadcasted_iota(jnp.int32, (1, slots), 1)
    info[0, 0] = ints[0, 0].astype(F32)
    info[0, 1] = ints[1, 0].astype(F32)
    info[0, 2] = jnp.where(slot_ids < cnt_ref[0, 0], wts[0], F32(0.0))
    for present, down in ((has_south, True), (has_north, False)):

        @pl.when(present)
        def _():
            info_copy(down).start()

    for f in range(fields):
        hal_send[0, 0, f : f + 1, :] = c_ref[f, rows - 1 : rows, :]
        hal_send[0, 1, f : f + 1, :] = c_ref[f, 0:1, :]
    stream = Stream(0, c_ref)

    zero_block = jnp.zeros((2, fields, rows, 128), F32)
    v_ref[:, :, :, 0:128] = zero_block
    v_ref[:, :, :, columns + 128 : columns + 256] = zero_block
    for present, slot in ((has_low, 0), (has_high, 1)):

        @pl.when(jnp.logical_not(present))
        def _():
            for ph in range(2):
                rad_buf[ph, slot] = jnp.zeros(rad_buf.shape[2:], F32)
                val_recv[ph, slot] = jnp.zeros(val_recv.shape[2:], F32)

    for present, slot in ((has_north, 0), (has_south, 1)):

        @pl.when(jnp.logical_not(present))
        def _():
            info[1 + slot] = jnp.zeros(info.shape[1:], F32)
            for ph in range(2):
                hal_recv[ph, slot] = jnp.zeros(hal_recv.shape[2:], F32)

    prepare(0)
    stream.step()
    stream.step()
    stream.step()
    for present, down in ((has_north, True), (has_south, False)):

        @pl.when(present)
        def _():
            info_copy(down).wait_recv()

    prepare(1)
    prepare(2)
    stream.step()
    overset(0, c_ref, stream)

    def pulled(e, cols, at, here, acc):
        value = STEP_SIZE * acc
        w_ref[e, :, cols] = value
        hal_send[1, 0, e : e + 1, cols] = value[rows - 1 : rows]
        hal_send[1, 1, e : e + 1, cols] = value[0:1]

    def first(k, carry):
        wait_chunk(0, c_ref, k)
        operator(0, k, pulled)
        return carry

    cuts = [0, min(4, chunks), min(6, chunks), chunks]
    lax.fori_loop(cuts[0], cuts[1], first, 0)
    stream.step()
    lax.fori_loop(cuts[1], cuts[2], first, 0)
    stream.finish()
    lax.fori_loop(cuts[2], cuts[3], first, 0)
    pack_border(1, w_ref)
    send_border(1)
    stream = Stream(1, w_ref)
    for _ in range(3):
        stream.step()
    overset(1, w_ref, stream)

    def final(e, cols, at, here, acc):
        out_ref[e, :, cols] = (
            v_ref[0, e, :, pl.ds(at + 128, BLK)] + here + (0.5 * STEP_SIZE) * acc
        )

    def second(k, carry):
        wait_chunk(1, w_ref, k)
        operator(1, k, final)
        cols = pl.ds(pl.multiple_of(k * width, width), width)
        pltpu.make_async_copy(
            out_ref.at[:, :, cols], out_hbm.at[:, :, cols], store_sem
        ).start()
        return carry

    lax.fori_loop(cuts[0], cuts[1], second, 0)
    stream.step()
    lax.fori_loop(cuts[1], cuts[2], second, 0)
    stream.finish()
    lax.fori_loop(cuts[2], cuts[3], second, 0)
    for present, down in ((has_south, True), (has_north, False)):

        @pl.when(present)
        def _():
            info_copy(down).wait_send()

    wait_sends(0)
    wait_sends(1)
    pltpu.make_async_copy(out_ref, out_hbm, store_sem).wait()


def body(
    final_cotangent,
    diffusivity,
    theta_velocity,
    phi_velocity,
    radial_stencil,
    field_coupling,
    slot_targets,
    slot_donors,
    slot_weights,
    slot_counts,
):
    fields, _, rows, columns = final_cotangent.shape[1:]
    tiles, levels = lax.axis_size("hor"), lax.axis_size("rad")
    slots = slot_targets.shape[-1]
    nblk = columns // BLK
    chunks = nblk
    window = -(-3 * (columns // tiles) // 128) * 128
    block = (fields, rows, columns)
    smem = pl.BlockSpec(memory_space=pltpu.SMEM)
    hbm = pl.BlockSpec(memory_space=pltpu.HBM)
    dma = pltpu.SemaphoreType.DMA
    out = pl.pallas_call(
        functools.partial(kernel, tiles, levels, chunks),
        out_shape=jax.ShapeDtypeStruct(block, F32),
        in_specs=[hbm, hbm, hbm, hbm, smem, smem, hbm, hbm, hbm, smem],
        out_specs=hbm,
        scratch_shapes=[
            pltpu.VMEM(block, F32),
            pltpu.VMEM(block, F32),
            pltpu.VMEM((3, rows, columns), F32),
            pltpu.VMEM((2, 1, 1, slots), jnp.int32),
            pltpu.VMEM((1, 1, slots), F32),
            pltpu.VMEM(block, F32),
            pltpu.VMEM((2, fields, rows, columns + 256), F32),
            pltpu.VMEM((2, 2, *block), F32),
            pltpu.VMEM((2, 2, fields, columns), F32),
            pltpu.VMEM((2, 2, fields, columns), F32),
            pltpu.VMEM((2, 1, 128), F32),
            pltpu.VMEM((2, tiles, 1, 128), F32),
            pltpu.VMEM((fields, columns + 384), F32),
            pltpu.VMEM((2, tiles, fields, window), F32),
            pltpu.VMEM((2, 2, fields, window), F32),
            pltpu.VMEM((2, fields, slots), F32),
            pltpu.VMEM((2, 2, fields, slots), F32),
            pltpu.VMEM((3, 3, 1, slots), F32),
            pltpu.VMEM((2 * window, 3 * slots), BF16),
            pltpu.VMEM((tiles, 3 * slots), BF16),
            pltpu.VMEM((1, 3 * slots), jnp.int32),
            pltpu.VMEM((3, 1, slots), jnp.int32),
            pltpu.VMEM((3, 2 * slots, BLK), BF16),
            pltpu.VMEM((nblk * fields * rows, 2 * slots), BF16),
            pltpu.VMEM((nblk * fields * rows, BLK), F32),
            pltpu.VMEM((nblk * fields * rows, BLK), F32),
            pltpu.VMEM((2, nblk * fields, BLK), F32),
            dma((7,)),
            dma(()),
            dma((2, 2, chunks)),
            dma((2, 2, chunks)),
            dma((2, 2, chunks)),
            dma((2, 2, chunks)),
            dma((2,)),
            dma((2,)),
            dma((2,)),
            dma((2, 2)),
            dma((2, 2)),
            dma((2, 2)),
            dma((2,)),
            dma((2,)),
        ],
        compiler_params=pltpu.CompilerParams(
            collective_id=0, has_side_effects=True, vmem_limit_bytes=60 * 2**20
        ),
        cost_estimate=pl.CostEstimate(
            flops=8_000_000, bytes_accessed=1_500_000, transcendentals=0
        ),
    )(
        final_cotangent.reshape(block),
        diffusivity,
        theta_velocity,
        phi_velocity,
        jnp.swapaxes(radial_stencil, 1, 2),
        field_coupling,
        slot_targets,
        slot_donors,
        slot_weights,
        slot_counts,
    )
    return out.reshape(final_cotangent.shape)


def solution(mesh):
    return jax.shard_map(
        body,
        mesh=mesh,
        in_specs=(
            P("panel", None, "rad", "hor", None),
            P("panel", "rad", "hor", None),
            P("panel", "rad", "hor", None),
            P("panel", "rad", "hor", None),
            P(),
            P(),
            P("panel", "hor", None),
            P("panel", "hor", None),
            P("panel", "hor", None),
            P("panel", "hor"),
        ),
        out_specs=P("panel", None, "rad", "hor", None),
        check_vma=False,
    )
```
